512 devices in a mesh: wide: 128 (over z, y, core), narrow: 4 (over x).
Axes of the slice: x: 4, y: 8, z: 8, core: 2. Of those that a mesh axis runs over, the one named last changes fastest.
Arguments:
- rhs: float32 [2048, 32, 128], P('wide', 'narrow'), may hold values from -4 to 6
- coefficient: float32 [2048, 32, 128], P('wide', 'narrow'), may hold values from 0.125 to 8
- guess: float32 [2048, 32, 128], P('wide', 'narrow'), may hold values from -6 to 6
Outputs:
- pressure: float32 [2048, 32, 128], P('wide', 'narrow')
- residual: float32 [2048, 32, 128], P('wide', 'narrow')
The draws below stay inside these ranges and needn't reach their ends.
All inputs are finite; a program needn't handle non-finite values.
Results may differ from the reference program's by a relative error of at most 0.0003.
Values sent between devices are 32-bit elements; how exact they have to be, the bound alone decides.
No kernel may reach another device: no remote copies, remote signals or barrier semaphores. Data moves between devices by JAX's collectives and lax.ppermute only.
A program may use at most 128 MiB of HBM per device.

```python
import math
import jax
import jax.numpy as jnp
from jax import lax

NY = 128
ITERS = 20
NX = 2048
NZ = 32


def position_x():
    return (lax.broadcasted_iota(jnp.float32, (NX, NZ, NY), 0) + 0.5) / NX


def draw_coefficient(key, part):
    key = jax.random.fold_in(key, 11)
    place = position_x()
    ramp = jnp.exp(math.log(4.0) * (2.0 * place - 1.0))
    rough = jnp.exp(jax.random.uniform(key, (NX, NZ, NY), jnp.float32, math.log(0.5), math.log(2.0)))
    return ramp * rough


def draw_rhs(key, part):
    key = jax.random.fold_in(key, 23)
    place = position_x()
    smooth_part = 1.0 + 0.5 * jnp.cos(2.0 * math.pi * place)
    rough = jnp.clip(jax.random.normal(key, (NX, NZ, NY), jnp.float32), -4.0, 4.0) * 0.9
    return jnp.clip(rough + smooth_part, -4.0, 6.0)


def block_scale(stream_key, dims, shards, low, top_value):
    level = 1.0
    for position, parts in shards:
        heights = jax.random.uniform(jax.random.fold_in(jax.random.fold_in(stream_key, 6), position), (parts,), jnp.float32, low / len(shards), top_value / len(shards))
        level = level * jnp.repeat(jnp.exp(heights), dims[position] // parts).reshape((-1,) + (1,) * (len(dims) - 1 - position))
    return level


def normal_values(stream_key, shape, scale, most, shards=(), kind=jnp.bfloat16):
    entries = jax.random.normal(stream_key, shape, jnp.float32) * scale
    if len(shards) > 0:
        entries = block_scale(stream_key, shape, shards, -0.22, 0.18) * entries
    return jnp.clip(entries, min=-most, max=most).astype(kind)


def setup_inputs(seed: int = 0) -> dict:
    key_list = jax.random.split(jax.random.key(seed), 4)
    return {
        "rhs": draw_rhs(jax.random.fold_in(key_list[3], 71), 0),
        "coefficient": draw_coefficient(jax.random.fold_in(key_list[3], 71), 0),
        "guess": normal_values(key_list[2], (NX, NZ, NY), 1.0, 6.0, ((0, 128), (1, 4)), jnp.float32),
    }


def shifts(field):
    padded = jnp.pad(field, 1)
    return [padded[2:, 1:-1, 1:-1], padded[:-2, 1:-1, 1:-1], padded[1:-1, 2:, 1:-1],
            padded[1:-1, :-2, 1:-1], padded[1:-1, 1:-1, 2:], padded[1:-1, 1:-1, :-2]]


def weights(conduct):
    faces = [0.5 * (conduct + other) for other in shifts(conduct)]
    total = faces[0]
    for face in faces[1:]:
        total = total + face
    return faces, total


def beside_all(faces, field):
    near = shifts(field)
    total = faces[0] * near[0]
    for index in range(1, 6):
        total = total + faces[index] * near[index]
    return total


def restrict(field):
    sx, sz, sy = field.shape
    return jnp.sum(field.reshape(sx // 2, 2, sz // 2, 2, sy // 2, 2), axis=(1, 3, 5)) * 0.125


def prolong(field):
    return jnp.repeat(jnp.repeat(jnp.repeat(field, 2, axis=0), 2, axis=1), 2, axis=2)


def colours(shape):
    return (lax.broadcasted_iota(jnp.int32, shape, 0) + lax.broadcasted_iota(jnp.int32, shape, 1)
            + lax.broadcasted_iota(jnp.int32, shape, 2)) % 2


def smooth(field, source, faces, diag, scale, colour):
    for sweep in range(2):
        for parity in (0, 1):
            fresh = (source / scale + beside_all(faces, field)) / diag
            field = jnp.where(colour == parity, fresh, field)
    return field


def defect(field, source, faces, diag, scale):
    return source - scale * (diag * field - beside_all(faces, field))


def bottom(source, faces, diag, scale):
    def advance(step, carry):
        answer, remain, search, norm_now = carry
        image = scale * (diag * search - beside_all(faces, search))
        alpha = norm_now / jnp.sum(search * image)
        answer = answer + alpha * search
        remain = remain - alpha * image
        norm_next = jnp.sum(remain * remain)
        search = remain + (norm_next / norm_now) * search
        return answer, remain, search, norm_next
    start = (jnp.zeros_like(source), source, source, jnp.sum(source * source))
    return lax.fori_loop(0, ITERS, advance, start)[0]


def reference(rhs, coefficient, guess):
    conducts = [coefficient]
    for level in range(3):
        conducts.append(restrict(conducts[-1]))
    operators = [weights(conduct) for conduct in conducts]
    field = guess
    source = rhs
    fields = []
    sources = []
    for level in range(3):
        scale = 0.25 ** level
        if level > 0:
            field = jnp.zeros_like(source)
        faces, diag = operators[level]
        colour = colours(source.shape)
        field = smooth(field, source, faces, diag, scale, colour)
        fields.append(field)
        sources.append(source)
        source = restrict(defect(field, source, faces, diag, scale))
    faces, diag = operators[3]
    correction = bottom(source, faces, diag, 0.25 ** 3)
    for level in (2, 1, 0):
        scale = 0.25 ** level
        faces, diag = operators[level]
        field = fields[level] + prolong(correction)
        field = smooth(field, sources[level], faces, diag, scale, colours(field.shape))
        correction = field
    faces, diag = operators[0]
    return field, defect(field, rhs, faces, diag, 1.0)
```

```python
import jax
import jax.numpy as jnp
from jax import lax
from jax.experimental import pallas as pl
from jax.experimental.pallas import tpu as pltpu
from jax.sharding import PartitionSpec as P

ITERS = 20
LANES = 128


class Level:
    def __init__(self, depth, pairs, rows, weights, beside):
        self.pairs, self.rows, self.step = pairs, rows, 1 << depth
        self.scale = 0.25**depth
        self.weights, self.beside = weights, beside
        z = lax.broadcasted_iota(jnp.int32, (rows, LANES), 0)
        lane = lax.broadcasted_iota(jnp.int32, (rows, LANES), 1)
        y = lane // self.step
        self.odd = (z + y) % 2 == 1
        self.y_odd = y % 2 == 1
        self.z_last, self.z_first = z == rows - 1, z == 0
        self.y_last, self.y_first = lane >= LANES - self.step, lane < self.step

    def other(self, colour, ref, i):
        after, before = ref[i + 1], ref[i - 1]
        return jnp.where(self.odd, after, before) if colour == 0 else jnp.where(self.odd, before, after)

    def rolled(self, value):
        return (
            pltpu.roll(value, self.rows - 1, 0),
            pltpu.roll(value, 1, 0),
            pltpu.roll(value, LANES - self.step, 1),
            pltpu.roll(value, self.step, 1),
        )

    def setup(self, conduct, low, high, first, count):
        edges = (self.z_last, self.z_first, self.y_last, self.y_first)

        def body(i):
            inside = jnp.logical_and(first + i >= 0, first + i < count)
            for colour in (0, 1):
                own, near = conduct[colour][i], conduct[1 - colour][i]
                same = 0.5 * (own + near)
                across = 0.5 * (own + self.other(colour, conduct[1 - colour], i))
                total = same + across
                if colour == 0:
                    self.beside[i] = same
                self.weights[colour, 0, i] = across
                for slot, (edge, value) in enumerate(zip(edges, self.rolled(near))):
                    face = 0.5 * (own + jnp.where(edge, 0.0, value))
                    total = total + face
                    self.weights[colour, 1 + slot, i] = jnp.where(edge, 0.0, face)
                self.weights[colour, 5, i] = total
                total = jnp.where(total > 0.0, total, 1.0)
                self.weights[colour, 6, i] = jnp.where(inside, 1.0 / total, 0.0)

        loop(low, high, body)

    def around(self, colour, field, i):
        near = field[1 - colour][i]
        total = self.beside[i] * near + self.weights[colour, 0, i] * self.other(colour, field[1 - colour], i)
        for slot, value in enumerate(self.rolled(near)):
            total = total + self.weights[colour, 1 + slot, i] * value
        return total

    def half(self, colour, field, source, low, high):
        def body(i):
            fresh = source[colour][i] + self.around(colour, field, i)
            field[colour][i] = fresh * self.weights[colour, 6, i]

        loop(low, high, body)

    def start(self, field, source, low, high):
        def body(i):
            field[0][i] = source[0][i] * self.weights[0, 6, i]

        loop(low, high, body)

    def defect(self, colour, field, source, i):
        rest = source[colour][i] + self.around(colour, field, i) - self.weights[colour, 5, i] * field[colour][i]
        return rest if self.scale == 1.0 else self.scale * rest

    def pair_sum(self, value):
        return value + jnp.where(self.y_odd, pltpu.roll(value, self.step, 1), pltpu.roll(value, LANES - self.step, 1))


def loop(low, high, body, group=2):
    whole = (high - low) // group * group
    if whole:

        def several(step, carry):
            for k in range(group):
                body(low + step * group + k)
            return carry

        lax.fori_loop(0, whole // group, several, 0)
    for i in range(low + whole, high):
        body(i)


def halved(ref, i, rows):
    return ref[i, pl.ds(0, rows // 2, 2), :] + ref[i, pl.ds(1, rows // 2, 2), :]


def zeroed(*refs):
    for ref in refs:
        ref[...] = jnp.zeros(ref.shape, ref.dtype)


def first_kernel(left, own, right, slab, one, two, weights0, beside0, weights1, beside1, buf1, sums, sums1, tmp):
    wide = lax.axis_index("wide")
    k0, f0, u0 = [(slab.at[2 * a], slab.at[2 * a + 1]) for a in range(3)]
    fine = Level(0, 24, 32, weights0, beside0)
    zeroed(u0[0])
    odd8 = fine.odd[:8]
    for base, part in ((0, left), (8, own), (16, right)):
        for n in range(4):
            z = slice(8 * n, 8 * n + 8)

            def unpack(i, part=part, n=n, z=z, base=base):
                for group, target in ((0, k0), (16, f0)):
                    even, uneven = part[n, group + 2 * i], part[n, group + 2 * i + 1]
                    target[0][base + i, z] = jnp.where(odd8, uneven, even)
                    target[1][base + i, z] = jnp.where(odd8, even, uneven)
                u0[1][base + i, z] = part[n, 32 + i]

            loop(0, 8, unpack)
    fine.setup(k0, 2, 22, 8 * wide - 8, 8 * lax.axis_size("wide"))
    fine.half(0, u0, f0, 2, 22)
    fine.half(1, u0, f0, 2, 22)
    fine.half(0, u0, f0, 3, 21)
    fine.half(1, u0, f0, 3, 21)

    def down_k(i):
        sums[i] = fine.pair_sum(k0[0][i] + k0[1][i])

    loop(2, 22, down_k)

    def down_f(i):
        sums1[i] = fine.pair_sum(fine.defect(0, u0, f0, i) + fine.defect(1, u0, f0, i))

    loop(4, 20, down_f)

    mid = Level(1, 12, 16, weights1, beside1)
    k1, f1, u1 = [(buf1.at[2 * a], buf1.at[2 * a + 1]) for a in range(3)]
    zeroed(u1[0], u1[1])

    def pack(target, source, factor, j):
        even, uneven = factor * halved(source, 2 * j, 32), factor * halved(source, 2 * j + 1, 32)
        target[0][j] = jnp.where(mid.odd, uneven, even)
        target[1][j] = jnp.where(mid.odd, even, uneven)

    loop(1, 11, lambda j: pack(k1, sums, 0.125, j))
    loop(2, 10, lambda j: pack(f1, sums1, 0.125 / 0.25, j))
    mid.setup(k1, 2, 10, 4 * wide - 4, 4 * lax.axis_size("wide"))
    mid.start(u1, f1, 2, 10)
    mid.half(1, u1, f1, 2, 10)
    mid.half(0, u1, f1, 3, 9)
    mid.half(1, u1, f1, 3, 9)
    for a in range(6):
        one[a] = buf1[a, 4:8]

    z8 = lax.broadcasted_iota(jnp.int32, (8, LANES), 0)
    lane8 = lax.broadcasted_iota(jnp.int32, (8, LANES), 1)
    odd2 = (z8 + lane8 // 4) % 2 == 1
    cells_k, cells_f = [], []
    for x in range(4):
        j = 4 + x
        tmp[2 * x] = mid.pair_sum(k1[0][j] + k1[1][j])
        tmp[2 * x + 1] = mid.pair_sum(mid.defect(0, u1, f1, j) + mid.defect(1, u1, f1, j))
        cells_k.append(0.125 * halved(tmp, 2 * x, 16))
        cells_f.append(0.125 / 0.0625 * halved(tmp, 2 * x + 1, 16))
    for t in range(2):
        for base, cells in ((0, cells_k), (2, cells_f)):
            even, uneven = cells[2 * t], cells[2 * t + 1]
            two[base, t] = jnp.where(odd2, uneven, even)
            two[base + 1, t] = jnp.where(odd2, even, uneven)


def second_kernel(*refs):
    parts, (slab, out, weights, beside) = refs[:7], refs[7:]
    wide = lax.axis_index("wide")
    level = Level(2, 16, 8, weights, beside)
    k, f, u = [(slab.at[2 * a], slab.at[2 * a + 1]) for a in range(3)]
    zeroed(slab)
    for place, part in enumerate(parts):
        for t in range(2):
            for a in range(4):
                slab[a, 1 + 2 * place + t] = part[a, t]
    level.setup(k, 1, 15, 2 * wide - 7, 2 * lax.axis_size("wide"))
    level.start(u, f, 1, 15)
    level.half(1, u, f, 2, 14)
    level.half(0, u, f, 2, 14)
    level.half(1, u, f, 3, 13)
    lane = lax.broadcasted_iota(jnp.int32, (8, LANES), 1)
    row = lax.broadcasted_iota(jnp.int32, (8, LANES), 0)
    pick = 8 * (lane % 16)
    keep = row == 2 * ((lane // 16) % 4)

    def compact(values):
        outs = []
        for value in values:
            value = level.pair_sum(value)
            value = 0.125 * (value + pltpu.roll(value, 7, 0))
            value = jnp.take_along_axis(value, pick, axis=1)
            outs.append(jnp.sum(jnp.where(keep, value, 0.0), axis=0, keepdims=True))
        return jnp.where(lane[:1] < 64, outs[0], outs[1])

    source = compact([level.defect(0, u, f, i) + level.defect(1, u, f, i) for i in (7, 8)])
    conduct = compact([k[0][i] + k[1][i] for i in (7, 8)])
    both = jnp.where(row % 2 == 0, source, conduct)
    for w in range(out.shape[0] // 8):
        out[8 * w : 8 * w + 8] = both


def coarsest(data, answer, remain, search, faces, iters):
    count = data.shape[0] // 2
    scale = 0.25**3
    row = lax.broadcasted_iota(jnp.int32, (count, LANES), 0)
    lane = lax.broadcasted_iota(jnp.int32, (count, LANES), 1)
    y, z, x = lane % 16, (lane // 16) % 4, lane // 64

    def around(value):
        swapped = pltpu.roll(value, 64, 1)
        across = jnp.where(x == 0, pltpu.roll(swapped, 1, 0), pltpu.roll(swapped, count - 1, 0))
        return (
            swapped,
            across,
            pltpu.roll(value, LANES - 16, 1),
            pltpu.roll(value, 16, 1),
            pltpu.roll(value, LANES - 1, 1),
            pltpu.roll(value, 1, 1),
        )

    source = data[pl.ds(0, count, 2), :]
    conduct = data[pl.ds(1, count, 2), :]
    edges = (
        None,
        jnp.logical_or(jnp.logical_and(x == 0, row == 0), jnp.logical_and(x == 1, row == count - 1)),
        z == 3,
        z == 0,
        y == 15,
        y == 0,
    )
    total = None
    for slot, (edge, value) in enumerate(zip(edges, around(conduct))):
        if edge is not None:
            value = jnp.where(edge, 0.0, value)
        face = (0.5 * scale) * (conduct + value)
        total = face if total is None else total + face
        faces[slot] = face if edge is None else jnp.where(edge, 0.0, face)
    faces[6] = total
    answer[...] = jnp.zeros_like(source)
    remain[...] = source
    search[...] = source

    def advance(step, norm):
        now = search[...]
        image = faces[6] * now
        for slot, value in enumerate(around(now)):
            image = image - faces[slot] * value
        alpha = norm / jnp.sum(now * image, axis=(0, 1), keepdims=True)
        answer[...] = answer[...] + alpha * now
        rest = remain[...] - alpha * image
        remain[...] = rest
        following = jnp.sum(rest * rest, axis=(0, 1), keepdims=True)
        search[...] = rest + (following / norm) * now
        return following

    lax.fori_loop(0, iters, advance, jnp.sum(source * source, axis=(0, 1), keepdims=True))


def third_kernel(data, slab2, left1, own1, right1, slab0, pressure, residual, answer, remain, search, faces,
                 weights2, beside2, u2, weights1, beside1, buf1, grow1, weights0, beside0, u0, grow0):
    wide, narrow = lax.axis_index("wide"), lax.axis_index("narrow")
    size = lax.axis_size("wide")
    zeroed(answer)
    coarsest(data, answer.at[pl.ds(8, data.shape[0] // 2)], remain, search, faces, ITERS)

    level = Level(2, 16, 8, weights2, beside2)
    k, f = [(slab2.at[2 * a], slab2.at[2 * a + 1]) for a in range(2)]
    zeroed(u2)
    lane = lax.broadcasted_iota(jnp.int32, (8, LANES), 1)
    row = lax.broadcasted_iota(jnp.int32, (8, LANES), 0)
    where_from = (row // 2) * 16 + lane // 8
    for t in range(5):
        line = answer[pl.ds(8 + wide - 2 + t, 1), :]
        line = jnp.broadcast_to(line, (8, LANES))
        for half in range(2):
            i = 3 + 2 * t + half
            u2[1, i] = slab2[5, i] + jnp.take_along_axis(line, where_from + 64 * half, axis=1)
    up2 = (u2.at[0], u2.at[1])
    level.setup(k, 3, 13, 2 * wide - 7, 2 * size)
    level.half(0, up2, f, 3, 13)
    level.half(1, up2, f, 4, 12)
    level.half(0, up2, f, 4, 12)
    level.half(1, up2, f, 5, 11)

    mid = Level(1, 12, 16, weights1, beside1)
    k1, f1, u1 = [(buf1.at[2 * a], buf1.at[2 * a + 1]) for a in range(3)]
    zeroed(u1[0])
    for a in (0, 1, 2, 3, 5):
        for place, part in enumerate((left1, own1, right1)):
            buf1[a, 4 * place : 4 * place + 4] = part[a]
    for j in range(12):
        i, side = 5 + j // 2, j % 2
        cell = jnp.where(level.odd, up2[1 - side][i], up2[side][i])
        grow1[j, pl.ds(0, 8, 2), :] = cell
        grow1[j, pl.ds(1, 8, 2), :] = cell
    for j in range(12):
        u1[1][j] = u1[1][j] + grow1[j]
    mid.setup(k1, 1, 11, 4 * wide - 4, 4 * size)
    mid.half(0, u1, f1, 1, 11)
    mid.half(1, u1, f1, 1, 11)
    mid.half(0, u1, f1, 2, 10)
    mid.half(1, u1, f1, 2, 10)

    fine = Level(0, 24, 32, weights0, beside0)
    k0, f0 = [(slab0.at[2 * a], slab0.at[2 * a + 1]) for a in range(2)]
    zeroed(u0.at[0])
    for i in range(5, 19):
        j, side = (i - 8 + 8) // 2, i % 2
        cell = jnp.where(mid.odd, u1[1 - side][j], u1[side][j])
        grow0[i, pl.ds(0, 16, 2), :] = cell
        grow0[i, pl.ds(1, 16, 2), :] = cell
    for i in range(5, 19):
        u0[1, i] = slab0[5, i] + grow0[i]
    up0 = (u0.at[0], u0.at[1])
    fine.setup(k0, 6, 18, 8 * wide - 8, 8 * size)
    fine.half(0, up0, f0, 6, 18)
    fine.half(1, up0, f0, 6, 18)
    fine.half(0, up0, f0, 7, 17)
    fine.half(1, up0, f0, 7, 17)
    odd8 = fine.odd[:8]

    def finish(i):
        grow0[0] = fine.defect(0, up0, f0, i)
        grow0[1] = fine.defect(1, up0, f0, i)
        rows = pl.ds(pl.multiple_of(8 * narrow, 8), 8)
        for out, first, second in (
            (pressure, u0[0, i, rows, :], u0[1, i, rows, :]),
            (residual, grow0[0, rows, :], grow0[1, rows, :]),
        ):
            out[2 * (i - 8)] = jnp.where(odd8, second, first)
            out[2 * (i - 8) + 1] = jnp.where(odd8, first, second)

    loop(8, 16, finish, group=1)


def f32(*shape):
    return jax.ShapeDtypeStruct(shape, jnp.float32)


def scratch(*shape):
    return pltpu.VMEM(shape, jnp.float32)


PARAMS = pltpu.CompilerParams(vmem_limit_bytes=48 * 1024 * 1024)


def shifted(block, distance):
    count = lax.axis_size("wide")
    if distance > 0:
        pairs = [(i, i + distance) for i in range(count - distance)]
    else:
        pairs = [(i, i + distance) for i in range(-distance, count)]
    return lax.ppermute(block, "wide", pairs)


def local(rhs, coefficient, guess):
    shape = (8, 8, LANES)
    odd = (lax.broadcasted_iota(jnp.int32, shape, 1) + lax.broadcasted_iota(jnp.int32, shape, 2)) % 2 == 1
    packed = jnp.where(odd, guess[0::2], guess[1::2])
    block = jnp.concatenate([coefficient, rhs, packed], axis=0)
    whole = lax.all_gather(block, "narrow")
    left, right = shifted(whole, 1), shifted(whole, -1)
    slab0, one, two = pl.pallas_call(
        first_kernel,
        out_shape=(f32(6, 24, 32, LANES), f32(6, 4, 16, LANES), f32(4, 2, 8, LANES)),
        scratch_shapes=[
            scratch(2, 7, 24, 32, LANES),
            scratch(24, 32, LANES),
            scratch(2, 7, 12, 16, LANES),
            scratch(12, 16, LANES),
            scratch(6, 12, 16, LANES),
            scratch(24, 32, LANES),
            scratch(24, 32, LANES),
            scratch(8, 16, LANES),
        ],
        compiler_params=PARAMS,
        name="first",
    )(left, whole, right)
    parts2 = [two if d == 0 else shifted(two, d) for d in (3, 2, 1, 0, -1, -2, -3)]
    left1, right1 = shifted(one, 1), shifted(one, -1)
    count = lax.axis_size("wide")
    slab2, out3 = pl.pallas_call(
        second_kernel,
        out_shape=(f32(6, 16, 8, LANES), f32(2 * count, LANES)),
        scratch_shapes=[scratch(2, 7, 16, 8, LANES), scratch(16, 8, LANES)],
        compiler_params=PARAMS,
        name="second",
    )(*parts2)
    data = lax.all_to_all(out3.reshape(count, 2, LANES), "wide", 0, 0).reshape(2 * count, LANES)
    return pl.pallas_call(
        third_kernel,
        out_shape=(f32(16, 8, LANES), f32(16, 8, LANES)),
        scratch_shapes=[
            scratch(count + 16, LANES),
            scratch(count, LANES),
            scratch(count, LANES),
            scratch(7, count, LANES),
            scratch(2, 7, 16, 8, LANES),
            scratch(16, 8, LANES),
            scratch(2, 16, 8, LANES),
            scratch(2, 7, 12, 16, LANES),
            scratch(12, 16, LANES),
            scratch(6, 12, 16, LANES),
            scratch(12, 16, LANES),
            scratch(2, 7, 24, 32, LANES),
            scratch(24, 32, LANES),
            scratch(2, 24, 32, LANES),
            scratch(24, 32, LANES),
        ],
        compiler_params=PARAMS,
        name="third",
    )(data, slab2, left1, one, right1, slab0)


def solution(mesh):
    spec = P("wide", "narrow", None)
    return jax.shard_map(
        local, mesh=mesh, in_specs=(spec, spec, spec), out_specs=(spec, spec), check_vma=False
    )
```

```python
import jax
import jax.numpy as jnp
from jax import lax
from jax.experimental import pallas as pl
from jax.experimental.pallas import tpu as pltpu
from jax.sharding import PartitionSpec as P

ITERS = 20
LANES = 128


class Level:
    def __init__(self, depth, pairs, rows, weights, beside):
        self.pairs, self.rows, self.step = pairs, rows, 1 << depth
        self.scale = 0.25**depth
        self.weights, self.beside = weights, beside
        z = lax.broadcasted_iota(jnp.int32, (rows, LANES), 0)
        lane = lax.broadcasted_iota(jnp.int32, (rows, LANES), 1)
        y = lane // self.step
        self.odd = (z + y) % 2 == 1
        self.y_odd = y % 2 == 1
        self.y_odd_lane = lane % 2 == 1
        self.z_last, self.z_first = z == rows - 1, z == 0
        self.y_last, self.y_first = lane >= LANES - self.step, lane < self.step

    def other(self, colour, ref, i):
        after, before = ref[i + 1], ref[i - 1]
        return jnp.where(self.odd, after, before) if colour == 0 else jnp.where(self.odd, before, after)

    def rolled(self, value):
        return (
            pltpu.roll(value, self.rows - 1, 0),
            pltpu.roll(value, 1, 0),
            pltpu.roll(value, LANES - self.step, 1),
            pltpu.roll(value, self.step, 1),
        )

    def setup(self, conduct, low, high, first, count):
        edges = (self.z_last, self.z_first, self.y_last, self.y_first)

        def body(i):
            inside = jnp.logical_and(first + i >= 0, first + i < count)
            for colour in (0, 1):
                own, near = conduct[colour][i], conduct[1 - colour][i]
                same = 0.5 * (own + near)
                across = 0.5 * (own + self.other(colour, conduct[1 - colour], i))
                total = same + across
                if colour == 0:
                    self.beside[i] = same
                self.weights[colour, 0, i] = across
                for slot, (edge, value) in enumerate(zip(edges, self.rolled(near))):
                    face = 0.5 * (own + jnp.where(edge, 0.0, value))
                    total = total + face
                    self.weights[colour, 1 + slot, i] = jnp.where(edge, 0.0, face)
                self.weights[colour, 5, i] = total
                total = jnp.where(total > 0.0, total, 1.0)
                self.weights[colour, 6, i] = jnp.where(inside, 1.0 / total, 0.0)

        loop(low, high, body)

    def around(self, colour, field, i):
        near = field[1 - colour][i]
        total = self.beside[i] * near + self.weights[colour, 0, i] * self.other(colour, field[1 - colour], i)
        for slot, value in enumerate(self.rolled(near)):
            total = total + self.weights[colour, 1 + slot, i] * value
        return total

    def half(self, colour, field, source, low, high):
        def body(i):
            fresh = source[colour][i] + self.around(colour, field, i)
            field[colour][i] = fresh * self.weights[colour, 6, i]

        loop(low, high, body)

    def start(self, field, source, low, high):
        def body(i):
            field[0][i] = source[0][i] * self.weights[0, 6, i]

        loop(low, high, body)

    def defect(self, colour, field, source, i):
        rest = source[colour][i] + self.around(colour, field, i) - self.weights[colour, 5, i] * field[colour][i]
        return rest if self.scale == 1.0 else self.scale * rest

    def pair_sum(self, value):
        return value + jnp.where(self.y_odd, pltpu.roll(value, self.step, 1), pltpu.roll(value, LANES - self.step, 1))


def loop(low, high, body, group=20):
    whole = (high - low) // group * group
    if whole:

        def several(step, carry):
            for k in range(group):
                body(low + step * group + k)
            return carry

        lax.fori_loop(0, whole // group, several, 0)
    for i in range(low + whole, high):
        body(i)


def halved(ref, i, rows):
    return ref[i, pl.ds(0, rows // 2, 2), :] + ref[i, pl.ds(1, rows // 2, 2), :]


def zeroed(*refs):
    for ref in refs:
        ref[...] = jnp.zeros(ref.shape, ref.dtype)


def first_kernel(left, own, right, slab, send, weights0, beside0, weights1, beside1, buf1, sums, sums1, tmp):
    wide = lax.axis_index("wide")
    k0, f0, u0 = [(slab.at[2 * a], slab.at[2 * a + 1]) for a in range(3)]
    fine = Level(0, 24, 32, weights0, beside0)
    zeroed(u0[0])
    odd8 = fine.odd[:8]
    for base, part in ((0, left), (8, own), (16, right)):
        for n in range(4):
            z = slice(8 * n, 8 * n + 8)

            def unpack(i, part=part, n=n, z=z, base=base):
                for group, target in ((0, k0), (16, f0)):
                    even, uneven = part[n, group + 2 * i], part[n, group + 2 * i + 1]
                    target[0][base + i, z] = jnp.where(odd8, uneven, even)
                    target[1][base + i, z] = jnp.where(odd8, even, uneven)
                u0[1][base + i, z] = part[n, 32 + i]

            loop(0, 8, unpack)
    fine.setup(k0, 2, 22, 8 * wide - 8, 8 * lax.axis_size("wide"))
    fine.half(0, u0, f0, 2, 22)
    fine.half(1, u0, f0, 2, 22)
    fine.half(0, u0, f0, 3, 21)
    fine.half(1, u0, f0, 3, 21)

    def down_k(i):
        sums[i] = fine.pair_sum(k0[0][i] + k0[1][i])

    loop(2, 22, down_k)

    def down_f(i):
        sums1[i] = fine.pair_sum(fine.defect(0, u0, f0, i) + fine.defect(1, u0, f0, i))

    loop(4, 20, down_f)

    mid = Level(1, 12, 16, weights1, beside1)
    k1, f1, u1 = [(buf1.at[2 * a], buf1.at[2 * a + 1]) for a in range(3)]
    zeroed(u1[0], u1[1])

    def pack(target, source, factor, j):
        even, uneven = factor * halved(source, 2 * j, 32), factor * halved(source, 2 * j + 1, 32)
        target[0][j] = jnp.where(mid.odd, uneven, even)
        target[1][j] = jnp.where(mid.odd, even, uneven)

    loop(1, 11, lambda j: pack(k1, sums, 0.125, j))
    loop(2, 10, lambda j: pack(f1, sums1, 0.125 / 0.25, j))
    mid.setup(k1, 2, 10, 4 * wide - 4, 4 * lax.axis_size("wide"))
    mid.start(u1, f1, 2, 10)
    mid.half(1, u1, f1, 2, 10)
    mid.half(0, u1, f1, 3, 9)
    mid.half(1, u1, f1, 3, 9)
    for slot, a in enumerate((0, 1, 2, 3, 5)):
        for t in range(2):
            both = jnp.where(mid.y_odd_lane, buf1[a, 5 + 2 * t], buf1[a, 4 + 2 * t])
            send[4 * slot + 2 * t : 4 * slot + 2 * t + 2] = both.reshape(2, 8, LANES)

    z8 = lax.broadcasted_iota(jnp.int32, (8, LANES), 0)
    lane8 = lax.broadcasted_iota(jnp.int32, (8, LANES), 1)
    odd2 = (z8 + lane8 // 4) % 2 == 1

    def write(base, cells):
        for t in range(len(cells) // 2):
            even, uneven = cells[2 * t], cells[2 * t + 1]
            send[base + t] = jnp.where(odd2, uneven, even)
            send[base + len(cells) // 2 + t] = jnp.where(odd2, even, uneven)

    for x in range(8):
        tmp[x] = mid.pair_sum(k1[0][2 + x] + k1[1][2 + x])
    for x in range(4):
        j = 4 + x
        tmp[8 + x] = mid.pair_sum(mid.defect(0, u1, f1, j) + mid.defect(1, u1, f1, j))
    write(20, [0.125 * halved(tmp, x, 16) for x in range(8)])
    write(28, [0.125 / 0.0625 * halved(tmp, 8 + x, 16) for x in range(4)])


def place_two(slab, part, base):
    for c in range(2):
        for t in range(4):
            slab[c, base - 1 + t] = part[20 + 4 * c + t]
        for t in range(2):
            slab[2 + c, base + t] = part[28 + 2 * c + t]


def second_kernel(left, own, right, out, near_low, near_high, slab, weights, beside):
    wide = lax.axis_index("wide")
    level = Level(2, 16, 8, weights, beside)
    k, f, u = [(slab.at[2 * a], slab.at[2 * a + 1]) for a in range(3)]
    zeroed(slab)
    place_two(slab, left, 5)
    place_two(slab, right, 9)
    place_two(slab, own, 7)
    for a in range(4):
        near_high[a] = slab[a, 5:9]
        near_low[a] = slab[a, 7:11]
    level.setup(k, 5, 11, 2 * wide - 7, 2 * lax.axis_size("wide"))
    level.start(u, f, 5, 11)
    level.half(1, u, f, 5, 11)
    level.half(0, u, f, 6, 10)
    level.half(1, u, f, 6, 10)
    lane = lax.broadcasted_iota(jnp.int32, (8, LANES), 1)
    row = lax.broadcasted_iota(jnp.int32, (8, LANES), 0)
    pick = 8 * (lane % 16)
    keep = row == 2 * ((lane // 16) % 4)

    def compact(values):
        outs = []
        for value in values:
            value = level.pair_sum(value)
            value = 0.125 * (value + pltpu.roll(value, 7, 0))
            value = jnp.take_along_axis(value, pick, axis=1)
            outs.append(jnp.sum(jnp.where(keep, value, 0.0), axis=0, keepdims=True))
        return jnp.where(lane[:1] < 64, outs[0], outs[1])

    source = compact([level.defect(0, u, f, i) + level.defect(1, u, f, i) for i in (7, 8)])
    conduct = compact([k[0][i] + k[1][i] for i in (7, 8)])
    both = jnp.where(row % 2 == 0, source, conduct)
    for w in range(out.shape[0] // 8):
        out[8 * w : 8 * w + 8] = both


def coarsest(data, answer, remain, search, image, faces, iters):
    parts = data.shape[0] // 16
    scale = 0.25**3
    row = lax.broadcasted_iota(jnp.int32, (8, LANES), 0)
    lane = lax.broadcasted_iota(jnp.int32, (8, LANES), 1)
    y, z, x = lane % 16, (lane // 16) % 4, lane // 64

    def around(values):
        swapped = [pltpu.roll(value, 64, 1) for value in values]
        before = [pltpu.roll(swapped[-1], 1, 0)] + swapped[:-1]
        after = swapped[1:] + [pltpu.roll(swapped[0], 7, 0)]
        return [
            (
                swapped[v],
                jnp.where(x == 0, before[v], after[v]),
                pltpu.roll(value, LANES - 16, 1),
                pltpu.roll(value, 16, 1),
                pltpu.roll(value, LANES - 1, 1),
                pltpu.roll(value, 1, 1),
            )
            for v, value in enumerate(values)
        ]

    def total(values):
        while len(values) > 1:
            values = [a + b for a, b in zip(values[::2], values[1::2])]
        value = values[0]
        for shift in (4, 2, 1):
            value = value + pltpu.roll(value, shift, 0)
        return jnp.sum(value, axis=1, keepdims=True)

    source = [data[pl.ds(2 * v, 8, 2 * parts), :] for v in range(parts)]
    conduct = [data[pl.ds(2 * v + 1, 8, 2 * parts), :] for v in range(parts)]
    for v, near in enumerate(around(conduct)):
        end = None
        if v == 0:
            end = jnp.logical_and(x == 0, row == 0)
        if v == parts - 1:
            end = jnp.logical_and(x == 1, row == 7)
        diagonal = None
        for slot, (edge, value) in enumerate(zip((None, end, z == 3, z == 0, y == 15, y == 0), near)):
            if edge is not None:
                value = jnp.where(edge, 0.0, value)
            face = (0.5 * scale) * (conduct[v] + value)
            diagonal = face if diagonal is None else diagonal + face
            faces[slot, v] = face if edge is None else jnp.where(edge, 0.0, face)
        faces[6, v] = diagonal

    def operate(values):
        return [
            faces[6, v] * values[v] - sum(faces[slot, v] * value for slot, value in enumerate(near))
            for v, near in enumerate(around(values))
        ]

    def products(values, images):
        return total([a * a for a in values]), total([a * b for a, b in zip(values, images)])

    first = operate(source)
    norm, power = products(source, first)
    alpha = norm / power
    for v in range(parts):
        answer[v] = alpha * source[v]
        remain[v] = source[v] - alpha * first[v]
        search[v] = source[v]
        image[v] = first[v]

    def advance(step, carry):
        norm, alpha = carry
        rest = [remain[v] for v in range(parts)]
        images = operate(rest)
        norm_next, power = products(rest, images)
        beta = norm_next / norm
        alpha = norm_next / (power - beta * norm_next / alpha)
        for v in range(parts):
            now = rest[v] + beta * search[v]
            search[v] = now
            out = images[v] + beta * image[v]
            image[v] = out
            answer[v] = answer[v] + alpha * now
            remain[v] = rest[v] - alpha * out
        return norm_next, alpha

    lax.fori_loop(0, iters - 1, advance, (norm, alpha))


def third_kernel(data, far_left, left, own, right, far_right, slab0, pressure, residual, answer, remain, search, image,
                 faces, weights2, beside2, slab2, weights1, beside1, buf1, grow1, weights0, beside0, u0, grow0):
    wide, narrow = lax.axis_index("wide"), lax.axis_index("narrow")
    size = lax.axis_size("wide")
    level = Level(2, 16, 8, weights2, beside2)
    k, f, up2 = [(slab2.at[2 * a], slab2.at[2 * a + 1]) for a in range(3)]
    zeroed(slab2)
    for a in range(4):
        slab2[a, 1:5] = far_left[a]
        slab2[a, 11:15] = far_right[a]
    place_two(slab2, left, 5)
    place_two(slab2, right, 9)
    place_two(slab2, own, 7)
    level.setup(k, 1, 15, 2 * wide - 7, 2 * size)
    level.start(up2, f, 1, 15)
    level.half(1, up2, f, 2, 14)
    level.half(0, up2, f, 2, 14)
    level.half(1, up2, f, 3, 13)

    coarsest(data, answer, remain, search, image, faces, ITERS)
    lane = lax.broadcasted_iota(jnp.int32, (8, LANES), 1)
    row = lax.broadcasted_iota(jnp.int32, (8, LANES), 0)
    where_from = (row // 2) * 16 + lane // 8
    parts = answer.shape[0]
    for t in range(5):
        at = wide - 2 + t
        inside = jnp.logical_and(at >= 0, at < size)
        at = jnp.clip(at, 0, size - 1)
        line = jnp.where(row == at // parts, answer[at % parts], 0.0)
        line = jnp.where(inside, jnp.sum(line, axis=0, keepdims=True), 0.0)
        line = jnp.broadcast_to(line, (8, LANES))
        for half in range(2):
            i = 3 + 2 * t + half
            slab2[5, i] = slab2[5, i] + jnp.take_along_axis(line, where_from + 64 * half, axis=1)
    level.half(0, up2, f, 3, 13)
    level.half(1, up2, f, 4, 12)
    level.half(0, up2, f, 4, 12)
    level.half(1, up2, f, 5, 11)

    mid = Level(1, 12, 16, weights1, beside1)
    k1, f1, u1 = [(buf1.at[2 * a], buf1.at[2 * a + 1]) for a in range(3)]
    zeroed(u1[0])
    for slot, a in enumerate((0, 1, 2, 3, 5)):
        for place, part in enumerate((left, own, right)):
            for t in range(2):
                both = part[4 * slot + 2 * t : 4 * slot + 2 * t + 2].reshape(16, LANES)
                j = 4 * place + 2 * t
                buf1[a, j] = jnp.where(mid.y_odd_lane, pltpu.roll(both, 1, 1), both)
                buf1[a, j + 1] = jnp.where(mid.y_odd_lane, both, pltpu.roll(both, LANES - 1, 1))
    for j in range(12):
        i, side = 5 + j // 2, j % 2
        cell = jnp.where(level.odd, up2[1 - side][i], up2[side][i])
        grow1[j, pl.ds(0, 8, 2), :] = cell
        grow1[j, pl.ds(1, 8, 2), :] = cell
    for j in range(12):
        u1[1][j] = u1[1][j] + grow1[j]
    mid.setup(k1, 1, 11, 4 * wide - 4, 4 * size)
    mid.half(0, u1, f1, 1, 11)
    mid.half(1, u1, f1, 1, 11)
    mid.half(0, u1, f1, 2, 10)
    mid.half(1, u1, f1, 2, 10)

    fine = Level(0, 24, 32, weights0, beside0)
    k0, f0 = [(slab0.at[2 * a], slab0.at[2 * a + 1]) for a in range(2)]
    zeroed(u0.at[0])
    for i in range(5, 19):
        j, side = (i - 8 + 8) // 2, i % 2
        cell = jnp.where(mid.odd, u1[1 - side][j], u1[side][j])
        grow0[i, pl.ds(0, 16, 2), :] = cell
        grow0[i, pl.ds(1, 16, 2), :] = cell
    for i in range(5, 19):
        u0[1, i] = slab0[5, i] + grow0[i]
    up0 = (u0.at[0], u0.at[1])
    fine.setup(k0, 6, 18, 8 * wide - 8, 8 * size)
    fine.half(0, up0, f0, 6, 18)
    fine.half(1, up0, f0, 6, 18)
    fine.half(0, up0, f0, 7, 17)
    fine.half(1, up0, f0, 7, 17)
    odd8 = fine.odd[:8]

    def finish(i):
        grow0[0] = fine.defect(0, up0, f0, i)
        grow0[1] = fine.defect(1, up0, f0, i)
        rows = pl.ds(pl.multiple_of(8 * narrow, 8), 8)
        for out, first, second in (
            (pressure, u0[0, i, rows, :], u0[1, i, rows, :]),
            (residual, grow0[0, rows, :], grow0[1, rows, :]),
        ):
            out[2 * (i - 8)] = jnp.where(odd8, second, first)
            out[2 * (i - 8) + 1] = jnp.where(odd8, first, second)

    loop(8, 16, finish, group=1)


def f32(*shape):
    return jax.ShapeDtypeStruct(shape, jnp.float32)


def scratch(*shape):
    return pltpu.VMEM(shape, jnp.float32)


PARAMS = pltpu.CompilerParams(vmem_limit_bytes=48 * 1024 * 1024)


def shifted(block, distance):
    count = lax.axis_size("wide")
    if distance > 0:
        pairs = [(i, i + distance) for i in range(count - distance)]
    else:
        pairs = [(i, i + distance) for i in range(-distance, count)]
    return lax.ppermute(block, "wide", pairs)


def local(rhs, coefficient, guess):
    shape = (8, 8, LANES)
    odd = (lax.broadcasted_iota(jnp.int32, shape, 1) + lax.broadcasted_iota(jnp.int32, shape, 2)) % 2 == 1
    packed = jnp.where(odd, guess[0::2], guess[1::2])
    block = jnp.concatenate([coefficient, rhs, packed], axis=0)
    whole = lax.all_gather(block, "narrow")
    left, right = shifted(whole, 1), shifted(whole, -1)
    slab0, send = pl.pallas_call(
        first_kernel,
        out_shape=(f32(6, 24, 32, LANES), f32(32, 8, LANES)),
        scratch_shapes=[
            scratch(2, 7, 24, 32, LANES),
            scratch(24, 32, LANES),
            scratch(2, 7, 12, 16, LANES),
            scratch(12, 16, LANES),
            scratch(6, 12, 16, LANES),
            scratch(24, 32, LANES),
            scratch(24, 32, LANES),
            scratch(12, 16, LANES),
        ],
        compiler_params=PARAMS,
        name="first",
    )(left, whole, right)
    near = (shifted(send, 1), send, shifted(send, -1))
    count = lax.axis_size("wide")
    out3, near_low, near_high = pl.pallas_call(
        second_kernel,
        out_shape=(f32(2 * count, LANES), f32(4, 4, 8, LANES), f32(4, 4, 8, LANES)),
        scratch_shapes=[scratch(6, 16, 8, LANES), scratch(2, 7, 16, 8, LANES), scratch(16, 8, LANES)],
        compiler_params=PARAMS,
        name="second",
    )(*near)
    far_left, far_right = shifted(near_high, 2), shifted(near_low, -2)
    data = lax.all_to_all(out3.reshape(count, 2, LANES), "wide", 0, 0).reshape(2 * count, LANES)
    return pl.pallas_call(
        third_kernel,
        out_shape=(f32(16, 8, LANES), f32(16, 8, LANES)),
        scratch_shapes=[
            scratch(count // 8, 8, LANES),
            scratch(count // 8, 8, LANES),
            scratch(count // 8, 8, LANES),
            scratch(count // 8, 8, LANES),
            scratch(7, count // 8, 8, LANES),
            scratch(2, 7, 16, 8, LANES),
            scratch(16, 8, LANES),
            scratch(6, 16, 8, LANES),
            scratch(2, 7, 12, 16, LANES),
            scratch(12, 16, LANES),
            scratch(6, 12, 16, LANES),
            scratch(12, 16, LANES),
            scratch(2, 7, 24, 32, LANES),
            scratch(24, 32, LANES),
            scratch(2, 24, 32, LANES),
            scratch(24, 32, LANES),
        ],
        compiler_params=PARAMS,
        name="third",
    )(data, far_left, *near, far_right, slab0)


def solution(mesh):
    spec = P("wide", "narrow", None)
    return jax.shard_map(
        local, mesh=mesh, in_specs=(spec, spec, spec), out_specs=(spec, spec), check_vma=False
    )
```

```python
import jax
import jax.numpy as jnp
from jax import lax
from jax.experimental import pallas as pl
from jax.experimental.pallas import tpu as pltpu
from jax.sharding import PartitionSpec as P

ITERS = 20
LANES = 128


class Level:
    def __init__(self, depth, pairs, rows, weights, beside):
        self.pairs, self.rows, self.step = pairs, rows, 1 << depth
        self.scale = 0.25**depth
        self.weights, self.beside = weights, beside
        z = lax.broadcasted_iota(jnp.int32, (rows, LANES), 0)
        lane = lax.broadcasted_iota(jnp.int32, (rows, LANES), 1)
        y = lane // self.step
        self.odd = (z + y) % 2 == 1
        self.y_odd = y % 2 == 1
        self.y_odd_lane = lane % 2 == 1
        self.z_last, self.z_first = z == rows - 1, z == 0
        self.y_last, self.y_first = lane >= LANES - self.step, lane < self.step

    def other(self, colour, ref, i):
        after, before = ref[i + 1], ref[i - 1]
        return jnp.where(self.odd, after, before) if colour == 0 else jnp.where(self.odd, before, after)

    def rolled(self, value):
        return (
            pltpu.roll(value, self.rows - 1, 0),
            pltpu.roll(value, 1, 0),
            pltpu.roll(value, LANES - self.step, 1),
            pltpu.roll(value, self.step, 1),
        )

    def setup(self, conduct, low, high, first, count):
        edges = (self.z_last, self.z_first, self.y_last, self.y_first)

        def body(i):
            inside = jnp.logical_and(first + i >= 0, first + i < count)
            for colour in (0, 1):
                own, near = conduct[colour][i], conduct[1 - colour][i]
                same = 0.5 * (own + near)
                across = 0.5 * (own + self.other(colour, conduct[1 - colour], i))
                total = same + across
                if colour == 0:
                    self.beside[i] = same
                self.weights[colour, 0, i] = across
                for slot, (edge, value) in enumerate(zip(edges, self.rolled(near))):
                    face = 0.5 * (own + jnp.where(edge, 0.0, value))
                    total = total + face
                    self.weights[colour, 1 + slot, i] = jnp.where(edge, 0.0, face)
                self.weights[colour, 5, i] = total
                total = jnp.where(total > 0.0, total, 1.0)
                self.weights[colour, 6, i] = jnp.where(inside, 1.0 / total, 0.0)

        loop(low, high, body)

    def around(self, colour, field, i):
        near = field[1 - colour][i]
        total = self.beside[i] * near + self.weights[colour, 0, i] * self.other(colour, field[1 - colour], i)
        for slot, value in enumerate(self.rolled(near)):
            total = total + self.weights[colour, 1 + slot, i] * value
        return total

    def half(self, colour, field, source, low, high):
        def body(i):
            fresh = source[colour][i] + self.around(colour, field, i)
            field[colour][i] = fresh * self.weights[colour, 6, i]

        loop(low, high, body)

    def start(self, field, source, low, high):
        def body(i):
            field[0][i] = source[0][i] * self.weights[0, 6, i]

        loop(low, high, body)

    def defect(self, colour, field, source, i):
        rest = source[colour][i] + self.around(colour, field, i) - self.weights[colour, 5, i] * field[colour][i]
        return rest if self.scale == 1.0 else self.scale * rest

    def pair_sum(self, value):
        return value + jnp.where(self.y_odd, pltpu.roll(value, self.step, 1), pltpu.roll(value, LANES - self.step, 1))


def loop(low, high, body, group=20):
    whole = (high - low) // group * group
    if whole:

        def several(step, carry):
            for k in range(group):
                body(low + step * group + k)
            return carry

        lax.fori_loop(0, whole // group, several, 0)
    for i in range(low + whole, high):
        body(i)


def halved(ref, i, rows):
    return ref[i, pl.ds(0, rows // 2, 2), :] + ref[i, pl.ds(1, rows // 2, 2), :]


def zeroed(*refs):
    for ref in refs:
        ref[...] = jnp.zeros(ref.shape, ref.dtype)


def spread_kernel(whole, to_right, to_left):
    for n in range(4):
        to_right[n, 0:13] = whole[n, 3:16]
        to_right[n, 13:25] = whole[n, 20:32]
        to_right[n, 25:32] = whole[n, 33:40]
        to_left[n, 0:13] = whole[n, 0:13]
        to_left[n, 13:25] = whole[n, 16:28]
        to_left[n, 25:32] = whole[n, 32:39]


def first_kernel(right, own, left, slab, send, weights0, beside0, weights1, beside1, buf1, sums, sums1, tmp):
    wide = lax.axis_index("wide")
    k0, f0, u0 = [(slab.at[2 * a], slab.at[2 * a + 1]) for a in range(3)]
    fine = Level(0, 24, 32, weights0, beside0)
    zeroed(u0[0])
    odd8 = fine.odd[:8]

    def row(base, n, kind, x):
        first, count = {"k": (0, 16), "f": (16, 16), "g": (32, 8)}[kind]
        start, kept = {"k": (0, 13), "f": (13, 12), "g": (25, 7)}[kind]
        if base == 8:
            return own[n, first + x]
        x = x - (count - kept) if base == 0 else x
        if x < 0 or x >= kept:
            return jnp.zeros((8, LANES), jnp.float32)
        return (left if base == 0 else right)[n, start + x]

    for n in range(4):
        z = slice(8 * n, 8 * n + 8)
        for i in range(1, 23):
            base, x = i // 8 * 8, 2 * (i % 8)
            for kind, target in (("k", k0), ("f", f0)):
                even, uneven = row(base, n, kind, x), row(base, n, kind, x + 1)
                target[0][i, z] = jnp.where(odd8, uneven, even)
                target[1][i, z] = jnp.where(odd8, even, uneven)
            u0[1][i, z] = row(base, n, "g", i % 8)
    fine.setup(k0, 2, 22, 8 * wide - 8, 8 * lax.axis_size("wide"))
    fine.half(0, u0, f0, 2, 22)
    fine.half(1, u0, f0, 2, 22)
    fine.half(0, u0, f0, 3, 21)
    fine.half(1, u0, f0, 3, 21)

    def down_k(i):
        sums[i] = fine.pair_sum(k0[0][i] + k0[1][i])

    loop(2, 22, down_k)

    def down_f(i):
        sums1[i] = fine.pair_sum(fine.defect(0, u0, f0, i) + fine.defect(1, u0, f0, i))

    loop(4, 20, down_f)

    mid = Level(1, 12, 16, weights1, beside1)
    k1, f1, u1 = [(buf1.at[2 * a], buf1.at[2 * a + 1]) for a in range(3)]
    zeroed(u1[0], u1[1])

    def pack(target, source, factor, j):
        even, uneven = factor * halved(source, 2 * j, 32), factor * halved(source, 2 * j + 1, 32)
        target[0][j] = jnp.where(mid.odd, uneven, even)
        target[1][j] = jnp.where(mid.odd, even, uneven)

    loop(1, 11, lambda j: pack(k1, sums, 0.125, j))
    loop(2, 10, lambda j: pack(f1, sums1, 0.125 / 0.25, j))
    mid.setup(k1, 2, 10, 4 * wide - 4, 4 * lax.axis_size("wide"))
    mid.start(u1, f1, 2, 10)
    mid.half(1, u1, f1, 2, 10)
    mid.half(0, u1, f1, 3, 9)
    mid.half(1, u1, f1, 3, 9)
    for slot, a in enumerate((0, 1, 2, 3, 5)):
        for t in range(2):
            both = jnp.where(mid.y_odd_lane, buf1[a, 5 + 2 * t], buf1[a, 4 + 2 * t])
            send[4 * slot + 2 * t : 4 * slot + 2 * t + 2] = both.reshape(2, 8, LANES)

    z8 = lax.broadcasted_iota(jnp.int32, (8, LANES), 0)
    lane8 = lax.broadcasted_iota(jnp.int32, (8, LANES), 1)
    odd2 = (z8 + lane8 // 4) % 2 == 1

    def write(base, cells):
        for t in range(len(cells) // 2):
            even, uneven = cells[2 * t], cells[2 * t + 1]
            send[base + t] = jnp.where(odd2, uneven, even)
            send[base + len(cells) // 2 + t] = jnp.where(odd2, even, uneven)

    for x in range(8):
        tmp[x] = mid.pair_sum(k1[0][2 + x] + k1[1][2 + x])
    for x in range(4):
        j = 4 + x
        tmp[8 + x] = mid.pair_sum(mid.defect(0, u1, f1, j) + mid.defect(1, u1, f1, j))
    write(20, [0.125 * halved(tmp, x, 16) for x in range(8)])
    write(28, [0.125 / 0.0625 * halved(tmp, 8 + x, 16) for x in range(4)])


def place_two(slab, part, base):
    for c in range(2):
        for t in range(4):
            slab[c, base - 1 + t] = part[20 + 4 * c + t]
        for t in range(2):
            slab[2 + c, base + t] = part[28 + 2 * c + t]


def second_kernel(left, own, right, out, near_low, near_high, slab, weights, beside):
    wide = lax.axis_index("wide")
    level = Level(2, 16, 8, weights, beside)
    k, f, u = [(slab.at[2 * a], slab.at[2 * a + 1]) for a in range(3)]
    zeroed(slab)
    place_two(slab, left, 5)
    place_two(slab, right, 9)
    place_two(slab, own, 7)
    for a in range(4):
        near_high[a] = slab[a, 5:9]
        near_low[a] = slab[a, 7:11]
    level.setup(k, 5, 11, 2 * wide - 7, 2 * lax.axis_size("wide"))
    level.start(u, f, 5, 11)
    level.half(1, u, f, 5, 11)
    level.half(0, u, f, 6, 10)
    level.half(1, u, f, 6, 10)
    lane = lax.broadcasted_iota(jnp.int32, (8, LANES), 1)
    row = lax.broadcasted_iota(jnp.int32, (8, LANES), 0)
    pick = 8 * (lane % 16)
    keep = row == 2 * ((lane // 16) % 4)

    def compact(values):
        outs = []
        for value in values:
            value = level.pair_sum(value)
            value = 0.125 * (value + pltpu.roll(value, 7, 0))
            value = jnp.take_along_axis(value, pick, axis=1)
            outs.append(jnp.sum(jnp.where(keep, value, 0.0), axis=0, keepdims=True))
        return jnp.where(lane[:1] < 64, outs[0], outs[1])

    source = compact([level.defect(0, u, f, i) + level.defect(1, u, f, i) for i in (7, 8)])
    conduct = compact([k[0][i] + k[1][i] for i in (7, 8)])
    both = jnp.where(row % 2 == 0, source, conduct)
    for w in range(out.shape[0] // 8):
        out[8 * w : 8 * w + 8] = both


def coarsest(data, answer, vectors, faces, iters):
    remain, search, image = (vectors.at[a] for a in range(3))
    parts = data.shape[0] // 16
    scale = 0.25**3
    row = lax.broadcasted_iota(jnp.int32, (8, LANES), 0)
    lane = lax.broadcasted_iota(jnp.int32, (8, LANES), 1)
    y, z, x = lane % 16, (lane // 16) % 4, lane // 64

    def around(values):
        swapped = [pltpu.roll(value, 64, 1) for value in values]
        before = [pltpu.roll(swapped[-1], 1, 0)] + swapped[:-1]
        after = swapped[1:] + [pltpu.roll(swapped[0], 7, 0)]
        return [
            (
                swapped[v],
                jnp.where(x == 0, before[v], after[v]),
                pltpu.roll(value, LANES - 16, 1),
                pltpu.roll(value, 16, 1),
                pltpu.roll(value, LANES - 1, 1),
                pltpu.roll(value, 1, 1),
            )
            for v, value in enumerate(values)
        ]

    def total(values):
        while len(values) > 1:
            values = [a + b for a, b in zip(values[::2], values[1::2])]
        value = values[0]
        for shift in (4, 2, 1):
            value = value + pltpu.roll(value, shift, 0)
        return jnp.sum(value, axis=1, keepdims=True)

    source = [data[pl.ds(2 * v, 8, 2 * parts), :] for v in range(parts)]
    conduct = [data[pl.ds(2 * v + 1, 8, 2 * parts), :] for v in range(parts)]
    for v, near in enumerate(around(conduct)):
        end = None
        if v == 0:
            end = jnp.logical_and(x == 0, row == 0)
        if v == parts - 1:
            end = jnp.logical_and(x == 1, row == 7)
        diagonal = None
        for slot, (edge, value) in enumerate(zip((None, end, z == 3, z == 0, y == 15, y == 0), near)):
            if edge is not None:
                value = jnp.where(edge, 0.0, value)
            face = (0.5 * scale) * (conduct[v] + value)
            diagonal = face if diagonal is None else diagonal + face
            faces[slot, v] = face if edge is None else jnp.where(edge, 0.0, face)
        faces[6, v] = diagonal

    def operate(values):
        return [
            faces[6, v] * values[v] - sum(faces[slot, v] * value for slot, value in enumerate(near))
            for v, near in enumerate(around(values))
        ]

    def products(values, images):
        return total([a * a for a in values]), total([a * b for a, b in zip(values, images)])

    def advance(step, carry):
        rest = [remain[v] for v in range(parts)]
        images = operate(rest)
        norm = total([a * a for a in rest])
        power = total([a * b for a, b in zip(rest, images)])
        if carry is None:
            for v in range(parts):
                answer[v] = jnp.zeros_like(rest[v])
        else:
            beta = norm * carry[0]
            power = power - beta * beta * carry[1]
        alpha = norm / power
        for v in range(parts):
            now, one = rest[v], images[v]
            if carry is not None:
                now, one = now + beta * search[v], one + beta * image[v]
            search[v], image[v] = now, one
            answer[v] = answer[v] + alpha * now
            remain[v] = rest[v] - alpha * one
        return 1.0 / norm, power

    for v, value in enumerate(source):
        remain[v] = value
    lax.fori_loop(0, iters - 1, advance, advance(0, None))


def third_kernel(data, far_left, left, own, right, far_right, slab0, pressure, residual, answer, vectors, faces,
                 weights2, beside2, slab2, weights1, beside1, buf1, grow1, weights0, beside0, u0, grow0):
    wide, narrow = lax.axis_index("wide"), lax.axis_index("narrow")
    size = lax.axis_size("wide")
    level = Level(2, 16, 8, weights2, beside2)
    k, f, up2 = [(slab2.at[2 * a], slab2.at[2 * a + 1]) for a in range(3)]
    zeroed(slab2)
    for a in range(4):
        slab2[a, 1:5] = far_left[a]
        slab2[a, 11:15] = far_right[a]
    place_two(slab2, left, 5)
    place_two(slab2, right, 9)
    place_two(slab2, own, 7)
    level.setup(k, 1, 15, 2 * wide - 7, 2 * size)
    level.start(up2, f, 1, 15)
    level.half(1, up2, f, 2, 14)
    level.half(0, up2, f, 2, 14)
    level.half(1, up2, f, 3, 13)

    coarsest(data, answer, vectors, faces, ITERS)
    lane = lax.broadcasted_iota(jnp.int32, (8, LANES), 1)
    row = lax.broadcasted_iota(jnp.int32, (8, LANES), 0)
    where_from = (row // 2) * 16 + lane // 8
    parts = answer.shape[0]
    for t in range(5):
        at = wide - 2 + t
        inside = jnp.logical_and(at >= 0, at < size)
        at = jnp.clip(at, 0, size - 1)
        line = jnp.where(row == at // parts, answer[at % parts], 0.0)
        line = jnp.where(inside, jnp.sum(line, axis=0, keepdims=True), 0.0)
        line = jnp.broadcast_to(line, (8, LANES))
        for half in range(2):
            i = 3 + 2 * t + half
            slab2[5, i] = slab2[5, i] + jnp.take_along_axis(line, where_from + 64 * half, axis=1)
    level.half(0, up2, f, 3, 13)
    level.half(1, up2, f, 4, 12)
    level.half(0, up2, f, 4, 12)
    level.half(1, up2, f, 5, 11)

    mid = Level(1, 12, 16, weights1, beside1)
    k1, f1, u1 = [(buf1.at[2 * a], buf1.at[2 * a + 1]) for a in range(3)]
    zeroed(u1[0])
    for slot, a in enumerate((0, 1, 2, 3, 5)):
        for place, part in enumerate((left, own, right)):
            for t in range(2):
                both = part[4 * slot + 2 * t : 4 * slot + 2 * t + 2].reshape(16, LANES)
                j = 4 * place + 2 * t
                buf1[a, j] = jnp.where(mid.y_odd_lane, pltpu.roll(both, 1, 1), both)
                buf1[a, j + 1] = jnp.where(mid.y_odd_lane, both, pltpu.roll(both, LANES - 1, 1))
    for j in range(12):
        i, side = 5 + j // 2, j % 2
        cell = jnp.where(level.odd, up2[1 - side][i], up2[side][i])
        grow1[j, pl.ds(0, 8, 2), :] = cell
        grow1[j, pl.ds(1, 8, 2), :] = cell
    for j in range(12):
        u1[1][j] = u1[1][j] + grow1[j]
    mid.setup(k1, 1, 11, 4 * wide - 4, 4 * size)
    mid.half(0, u1, f1, 1, 11)
    mid.half(1, u1, f1, 1, 11)
    mid.half(0, u1, f1, 2, 10)
    mid.half(1, u1, f1, 2, 10)

    fine = Level(0, 24, 32, weights0, beside0)
    k0, f0 = [(slab0.at[2 * a], slab0.at[2 * a + 1]) for a in range(2)]
    zeroed(u0.at[0])
    for i in range(5, 19):
        j, side = (i - 8 + 8) // 2, i % 2
        cell = jnp.where(mid.odd, u1[1 - side][j], u1[side][j])
        grow0[i, pl.ds(0, 16, 2), :] = cell
        grow0[i, pl.ds(1, 16, 2), :] = cell
    for i in range(5, 19):
        u0[1, i] = slab0[5, i] + grow0[i]
    up0 = (u0.at[0], u0.at[1])
    fine.setup(k0, 6, 18, 8 * wide - 8, 8 * size)
    fine.half(0, up0, f0, 6, 18)
    fine.half(1, up0, f0, 6, 18)
    fine.half(0, up0, f0, 7, 17)
    fine.half(1, up0, f0, 7, 17)
    odd8 = fine.odd[:8]

    def finish(i):
        grow0[0] = fine.defect(0, up0, f0, i)
        grow0[1] = fine.defect(1, up0, f0, i)
        rows = pl.ds(pl.multiple_of(8 * narrow, 8), 8)
        for out, first, second in (
            (pressure, u0[0, i, rows, :], u0[1, i, rows, :]),
            (residual, grow0[0, rows, :], grow0[1, rows, :]),
        ):
            out[2 * (i - 8)] = jnp.where(odd8, second, first)
            out[2 * (i - 8) + 1] = jnp.where(odd8, first, second)

    loop(8, 16, finish, group=1)


def f32(*shape):
    return jax.ShapeDtypeStruct(shape, jnp.float32)


def scratch(*shape):
    return pltpu.VMEM(shape, jnp.float32)


PARAMS = pltpu.CompilerParams(vmem_limit_bytes=48 * 1024 * 1024)


def shifted(block, distance):
    count = lax.axis_size("wide")
    if distance > 0:
        pairs = [(i, i + distance) for i in range(count - distance)]
    else:
        pairs = [(i, i + distance) for i in range(-distance, count)]
    return lax.ppermute(block, "wide", pairs)


def local(rhs, coefficient, guess):
    shape = (8, 8, LANES)
    odd = (lax.broadcasted_iota(jnp.int32, shape, 1) + lax.broadcasted_iota(jnp.int32, shape, 2)) % 2 == 1
    packed = jnp.where(odd, guess[0::2], guess[1::2])
    whole = lax.all_gather(jnp.concatenate([coefficient, rhs, packed], axis=0), "narrow")
    to_right, to_left = pl.pallas_call(
        spread_kernel,
        out_shape=(f32(4, 32, 8, LANES), f32(4, 32, 8, LANES)),
        compiler_params=PARAMS,
        name="spread",
    )(whole)
    right = shifted(to_left, -1)
    left = shifted(to_right, 1)
    slab0, send = pl.pallas_call(
        first_kernel,
        out_shape=(f32(6, 24, 32, LANES), f32(32, 8, LANES)),
        scratch_shapes=[
            scratch(2, 7, 24, 32, LANES),
            scratch(24, 32, LANES),
            scratch(2, 7, 12, 16, LANES),
            scratch(12, 16, LANES),
            scratch(6, 12, 16, LANES),
            scratch(24, 32, LANES),
            scratch(24, 32, LANES),
            scratch(12, 16, LANES),
        ],
        compiler_params=PARAMS,
        name="first",
    )(right, whole, left)
    near = (shifted(send, 1), send, shifted(send, -1))
    count = lax.axis_size("wide")
    out3, near_low, near_high = pl.pallas_call(
        second_kernel,
        out_shape=(f32(2 * count, LANES), f32(4, 4, 8, LANES), f32(4, 4, 8, LANES)),
        scratch_shapes=[scratch(6, 16, 8, LANES), scratch(2, 7, 16, 8, LANES), scratch(16, 8, LANES)],
        compiler_params=PARAMS,
        name="second",
    )(*near)
    far_left, far_right = shifted(near_high, 2), shifted(near_low, -2)
    data = lax.all_to_all(out3.reshape(count, 2, LANES), "wide", 0, 0).reshape(2 * count, LANES)
    return pl.pallas_call(
        third_kernel,
        out_shape=(f32(16, 8, LANES), f32(16, 8, LANES)),
        scratch_shapes=[
            scratch(count // 8, 8, LANES),
            scratch(3, count // 8, 8, LANES),
            scratch(7, count // 8, 8, LANES),
            scratch(2, 7, 16, 8, LANES),
            scratch(16, 8, LANES),
            scratch(6, 16, 8, LANES),
            scratch(2, 7, 12, 16, LANES),
            scratch(12, 16, LANES),
            scratch(6, 12, 16, LANES),
            scratch(12, 16, LANES),
            scratch(2, 7, 24, 32, LANES),
            scratch(24, 32, LANES),
            scratch(2, 24, 32, LANES),
            scratch(24, 32, LANES),
        ],
        compiler_params=PARAMS,
        name="third",
    )(data, far_left, *near, far_right, slab0)


def solution(mesh):
    spec = P("wide", "narrow", None)
    return jax.shard_map(
        local, mesh=mesh, in_specs=(spec, spec, spec), out_specs=(spec, spec), check_vma=False
    )
```

```python
import jax
import jax.numpy as jnp
from jax import lax
from jax.experimental import pallas as pl
from jax.experimental.pallas import tpu as pltpu
from jax.sharding import PartitionSpec as P

ITERS = 20
LANES = 128


class Level:
    def __init__(self, depth, pairs, rows, weights, beside):
        self.pairs, self.rows, self.step = pairs, rows, 1 << depth
        self.scale = 0.25**depth
        self.weights, self.beside = weights, beside
        z = lax.broadcasted_iota(jnp.int32, (rows, LANES), 0)
        lane = lax.broadcasted_iota(jnp.int32, (rows, LANES), 1)
        y = lane // self.step
        self.odd = (z + y) % 2 == 1
        self.y_odd = y % 2 == 1
        self.y_odd_lane = lane % 2 == 1
        self.z_last, self.z_first = z == rows - 1, z == 0
        self.y_last, self.y_first = lane >= LANES - self.step, lane < self.step

    def other(self, colour, ref, i):
        after, before = ref[i + 1], ref[i - 1]
        return jnp.where(self.odd, after, before) if colour == 0 else jnp.where(self.odd, before, after)

    def rolled(self, value):
        return (
            pltpu.roll(value, self.rows - 1, 0),
            pltpu.roll(value, 1, 0),
            pltpu.roll(value, LANES - self.step, 1),
            pltpu.roll(value, self.step, 1),
        )

    def setup(self, conduct, low, high, first, count):
        edges = (self.z_last, self.z_first, self.y_last, self.y_first)

        def body(i):
            inside = jnp.logical_and(first + i >= 0, first + i < count)
            for colour in (0, 1):
                own, near = conduct[colour][i], conduct[1 - colour][i]
                same = 0.5 * (own + near)
                across = 0.5 * (own + self.other(colour, conduct[1 - colour], i))
                total = same + across
                if colour == 0:
                    self.beside[i] = same
                self.weights[colour, 0, i] = across
                for slot, (edge, value) in enumerate(zip(edges, self.rolled(near))):
                    face = 0.5 * (own + jnp.where(edge, 0.0, value))
                    total = total + face
                    self.weights[colour, 1 + slot, i] = jnp.where(edge, 0.0, face)
                self.weights[colour, 5, i] = total
                total = jnp.where(total > 0.0, total, 1.0)
                self.weights[colour, 6, i] = jnp.where(inside, 1.0 / total, 0.0)

        loop(low, high, body)

    def around(self, colour, field, i):
        near = field[1 - colour][i]
        total = self.beside[i] * near + self.weights[colour, 0, i] * self.other(colour, field[1 - colour], i)
        for slot, value in enumerate(self.rolled(near)):
            total = total + self.weights[colour, 1 + slot, i] * value
        return total

    def half(self, colour, field, source, low, high):
        def body(i):
            fresh = source[colour][i] + self.around(colour, field, i)
            field[colour][i] = fresh * self.weights[colour, 6, i]

        loop(low, high, body)

    def start(self, field, source, low, high):
        def body(i):
            field[0][i] = source[0][i] * self.weights[0, 6, i]

        loop(low, high, body)

    def defect(self, colour, field, source, i):
        rest = source[colour][i] + self.around(colour, field, i) - self.weights[colour, 5, i] * field[colour][i]
        return rest if self.scale == 1.0 else self.scale * rest

    def pair_sum(self, value):
        return value + jnp.where(self.y_odd, pltpu.roll(value, self.step, 1), pltpu.roll(value, LANES - self.step, 1))


def loop(low, high, body, group=20):
    whole = (high - low) // group * group
    if whole:

        def several(step, carry):
            for k in range(group):
                body(low + step * group + k)
            return carry

        lax.fori_loop(0, whole // group, several, 0)
    for i in range(low + whole, high):
        body(i)


def halved(ref, i, rows):
    return ref[i, pl.ds(0, rows // 2, 2), :] + ref[i, pl.ds(1, rows // 2, 2), :]


def zeroed(*refs):
    for ref in refs:
        ref[...] = jnp.zeros(ref.shape, ref.dtype)


class Chosen:
    def __init__(self, which, yes, no):
        self.which, self.yes, self.no = which, yes, no

    def __getitem__(self, at):
        return jnp.where(self.which, self.yes[at], self.no[at])


def sides(abroad, home):
    even = lax.axis_index("wide") % 2 == 0
    return Chosen(even, abroad, home), Chosen(even, home, abroad)


def spread_kernel(whole, abroad, home):
    odd = lax.axis_index("wide") % 2
    for out, right in ((abroad, odd), (home, 1 - odd)):
        for n in range(4):
            out[n, 0:13] = whole[n, pl.ds(3 * right, 13)]
            out[n, 13:25] = whole[n, pl.ds(16 + 4 * right, 12)]
            out[n, 25:32] = whole[n, pl.ds(32 + right, 7)]


def first_kernel(abroad, own, home, slab, send, weights0, beside0, weights1, beside1, buf1, sums, sums1, tmp):
    wide = lax.axis_index("wide")
    left, right = sides(abroad, home)
    k0, f0, u0 = [(slab.at[2 * a], slab.at[2 * a + 1]) for a in range(3)]
    fine = Level(0, 24, 32, weights0, beside0)
    zeroed(u0[0])
    odd8 = fine.odd[:8]

    def row(base, n, kind, x):
        first, count = {"k": (0, 16), "f": (16, 16), "g": (32, 8)}[kind]
        start, kept = {"k": (0, 13), "f": (13, 12), "g": (25, 7)}[kind]
        if base == 8:
            return own[n, first + x]
        x = x - (count - kept) if base == 0 else x
        if x < 0 or x >= kept:
            return jnp.zeros((8, LANES), jnp.float32)
        return (left if base == 0 else right)[n, start + x]

    for n in range(4):
        z = slice(8 * n, 8 * n + 8)
        for i in range(1, 23):
            base, x = i // 8 * 8, 2 * (i % 8)
            for kind, target in (("k", k0), ("f", f0)):
                even, uneven = row(base, n, kind, x), row(base, n, kind, x + 1)
                target[0][i, z] = jnp.where(odd8, uneven, even)
                target[1][i, z] = jnp.where(odd8, even, uneven)
            u0[1][i, z] = row(base, n, "g", i % 8)
    fine.setup(k0, 2, 22, 8 * wide - 8, 8 * lax.axis_size("wide"))
    fine.half(0, u0, f0, 2, 22)
    fine.half(1, u0, f0, 2, 22)
    fine.half(0, u0, f0, 3, 21)
    fine.half(1, u0, f0, 3, 21)

    def down_k(i):
        sums[i] = fine.pair_sum(k0[0][i] + k0[1][i])

    loop(2, 22, down_k)

    def down_f(i):
        sums1[i] = fine.pair_sum(fine.defect(0, u0, f0, i) + fine.defect(1, u0, f0, i))

    loop(4, 20, down_f)

    mid = Level(1, 12, 16, weights1, beside1)
    k1, f1, u1 = [(buf1.at[2 * a], buf1.at[2 * a + 1]) for a in range(3)]
    zeroed(u1[0], u1[1])

    def pack(target, source, factor, j):
        even, uneven = factor * halved(source, 2 * j, 32), factor * halved(source, 2 * j + 1, 32)
        target[0][j] = jnp.where(mid.odd, uneven, even)
        target[1][j] = jnp.where(mid.odd, even, uneven)

    loop(1, 11, lambda j: pack(k1, sums, 0.125, j))
    loop(2, 10, lambda j: pack(f1, sums1, 0.125 / 0.25, j))
    mid.setup(k1, 2, 10, 4 * wide - 4, 4 * lax.axis_size("wide"))
    mid.start(u1, f1, 2, 10)
    mid.half(1, u1, f1, 2, 10)
    mid.half(0, u1, f1, 3, 9)
    mid.half(1, u1, f1, 3, 9)
    for slot, a in enumerate((0, 1, 2, 3, 5)):
        for t in range(2):
            both = jnp.where(mid.y_odd_lane, buf1[a, 5 + 2 * t], buf1[a, 4 + 2 * t])
            send[4 * slot + 2 * t : 4 * slot + 2 * t + 2] = both.reshape(2, 8, LANES)

    z8 = lax.broadcasted_iota(jnp.int32, (8, LANES), 0)
    lane8 = lax.broadcasted_iota(jnp.int32, (8, LANES), 1)
    odd2 = (z8 + lane8 // 4) % 2 == 1

    def write(base, cells):
        for t in range(len(cells) // 2):
            even, uneven = cells[2 * t], cells[2 * t + 1]
            send[base + t] = jnp.where(odd2, uneven, even)
            send[base + len(cells) // 2 + t] = jnp.where(odd2, even, uneven)

    for x in range(8):
        tmp[x] = mid.pair_sum(k1[0][2 + x] + k1[1][2 + x])
    for x in range(4):
        j = 4 + x
        tmp[8 + x] = mid.pair_sum(mid.defect(0, u1, f1, j) + mid.defect(1, u1, f1, j))
    write(20, [0.125 * halved(tmp, x, 16) for x in range(8)])
    write(28, [0.125 / 0.0625 * halved(tmp, 8 + x, 16) for x in range(4)])


def place_two(slab, part, base):
    for c in range(2):
        for t in range(4):
            slab[c, base - 1 + t] = part[20 + 4 * c + t]
        for t in range(2):
            slab[2 + c, base + t] = part[28 + 2 * c + t]


def second_kernel(home, own, abroad, out, near_low, near_high, slab, weights, beside):
    wide = lax.axis_index("wide")
    left, right = sides(abroad, home)
    level = Level(2, 16, 8, weights, beside)
    k, f, u = [(slab.at[2 * a], slab.at[2 * a + 1]) for a in range(3)]
    zeroed(slab)
    place_two(slab, left, 5)
    place_two(slab, right, 9)
    place_two(slab, own, 7)
    for a in range(4):
        near_high[a] = slab[a, 5:9]
        near_low[a] = slab[a, 7:11]
    level.setup(k, 5, 11, 2 * wide - 7, 2 * lax.axis_size("wide"))
    level.start(u, f, 5, 11)
    level.half(1, u, f, 5, 11)
    level.half(0, u, f, 6, 10)
    level.half(1, u, f, 6, 10)
    lane = lax.broadcasted_iota(jnp.int32, (8, LANES), 1)
    row = lax.broadcasted_iota(jnp.int32, (8, LANES), 0)
    pick = 8 * (lane % 16)
    keep = row == 2 * ((lane // 16) % 4)

    def compact(values):
        outs = []
        for value in values:
            value = level.pair_sum(value)
            value = 0.125 * (value + pltpu.roll(value, 7, 0))
            value = jnp.take_along_axis(value, pick, axis=1)
            outs.append(jnp.sum(jnp.where(keep, value, 0.0), axis=0, keepdims=True))
        return jnp.where(lane[:1] < 64, outs[0], outs[1])

    source = compact([level.defect(0, u, f, i) + level.defect(1, u, f, i) for i in (7, 8)])
    conduct = compact([k[0][i] + k[1][i] for i in (7, 8)])
    both = jnp.where(row % 2 == 0, source, conduct)
    for w in range(out.shape[0] // 8):
        out[8 * w : 8 * w + 8] = both


def coarsest(data, answer, vectors, faces, iters):
    remain, search, image = (vectors.at[a] for a in range(3))
    parts = data.shape[0] // 16
    scale = 0.25**3
    row = lax.broadcasted_iota(jnp.int32, (8, LANES), 0)
    lane = lax.broadcasted_iota(jnp.int32, (8, LANES), 1)
    y, z, x = lane % 16, (lane // 16) % 4, lane // 64

    def around(values):
        swapped = [pltpu.roll(value, 64, 1) for value in values]
        before = [pltpu.roll(swapped[-1], 1, 0)] + swapped[:-1]
        after = swapped[1:] + [pltpu.roll(swapped[0], 7, 0)]
        return [
            (
                swapped[v],
                jnp.where(x == 0, before[v], after[v]),
                pltpu.roll(value, LANES - 16, 1),
                pltpu.roll(value, 16, 1),
                pltpu.roll(value, LANES - 1, 1),
                pltpu.roll(value, 1, 1),
            )
            for v, value in enumerate(values)
        ]

    def total(values):
        while len(values) > 1:
            values = [a + b for a, b in zip(values[::2], values[1::2])]
        value = values[0]
        for shift in (4, 2, 1):
            value = value + pltpu.roll(value, shift, 0)
        return jnp.sum(value, axis=1, keepdims=True)

    source = [data[pl.ds(2 * v, 8, 2 * parts), :] for v in range(parts)]
    conduct = [data[pl.ds(2 * v + 1, 8, 2 * parts), :] for v in range(parts)]
    for v, near in enumerate(around(conduct)):
        end = None
        if v == 0:
            end = jnp.logical_and(x == 0, row == 0)
        if v == parts - 1:
            end = jnp.logical_and(x == 1, row == 7)
        diagonal = None
        for slot, (edge, value) in enumerate(zip((None, end, z == 3, z == 0, y == 15, y == 0), near)):
            if edge is not None:
                value = jnp.where(edge, 0.0, value)
            face = (0.5 * scale) * (conduct[v] + value)
            diagonal = face if diagonal is None else diagonal + face
            faces[slot, v] = face if edge is None else jnp.where(edge, 0.0, face)
        faces[6, v] = diagonal

    def operate(values):
        return [
            faces[6, v] * values[v] - sum(faces[slot, v] * value for slot, value in enumerate(near))
            for v, near in enumerate(around(values))
        ]

    def products(values, images):
        return total([a * a for a in values]), total([a * b for a, b in zip(values, images)])

    def advance(step, carry):
        rest = [remain[v] for v in range(parts)]
        images = operate(rest)
        norm = total([a * a for a in rest])
        power = total([a * b for a, b in zip(rest, images)])
        if carry is None:
            for v in range(parts):
                answer[v] = jnp.zeros_like(rest[v])
        else:
            beta = norm * carry[0]
            power = power - beta * beta * carry[1]
        alpha = norm / power
        for v in range(parts):
            now, one = rest[v], images[v]
            if carry is not None:
                now, one = now + beta * search[v], one + beta * image[v]
            search[v], image[v] = now, one
            answer[v] = answer[v] + alpha * now
            remain[v] = rest[v] - alpha * one
        return 1.0 / norm, power

    for v, value in enumerate(source):
        remain[v] = value
    lax.fori_loop(0, iters - 1, advance, advance(0, None))


def third_kernel(data, far_left, home, own, abroad, far_right, slab0, pressure, residual, answer, vectors, faces,
                 weights2, beside2, slab2, weights1, beside1, buf1, grow1, weights0, beside0, u0, grow0):
    wide, narrow = lax.axis_index("wide"), lax.axis_index("narrow")
    left, right = sides(abroad, home)
    size = lax.axis_size("wide")
    level = Level(2, 16, 8, weights2, beside2)
    k, f, up2 = [(slab2.at[2 * a], slab2.at[2 * a + 1]) for a in range(3)]
    zeroed(slab2)
    for a in range(4):
        slab2[a, 1:5] = far_left[a]
        slab2[a, 11:15] = far_right[a]
    place_two(slab2, left, 5)
    place_two(slab2, right, 9)
    place_two(slab2, own, 7)
    level.setup(k, 1, 15, 2 * wide - 7, 2 * size)
    level.start(up2, f, 1, 15)
    level.half(1, up2, f, 2, 14)
    level.half(0, up2, f, 2, 14)
    level.half(1, up2, f, 3, 13)

    coarsest(data, answer, vectors, faces, ITERS)
    lane = lax.broadcasted_iota(jnp.int32, (8, LANES), 1)
    row = lax.broadcasted_iota(jnp.int32, (8, LANES), 0)
    where_from = (row // 2) * 16 + lane // 8
    parts = answer.shape[0]
    for t in range(5):
        at = wide - 2 + t
        inside = jnp.logical_and(at >= 0, at < size)
        at = jnp.clip(at, 0, size - 1)
        line = jnp.where(row == at // parts, answer[at % parts], 0.0)
        line = jnp.where(inside, jnp.sum(line, axis=0, keepdims=True), 0.0)
        line = jnp.broadcast_to(line, (8, LANES))
        for half in range(2):
            i = 3 + 2 * t + half
            slab2[5, i] = slab2[5, i] + jnp.take_along_axis(line, where_from + 64 * half, axis=1)
    level.half(0, up2, f, 3, 13)
    level.half(1, up2, f, 4, 12)
    level.half(0, up2, f, 4, 12)
    level.half(1, up2, f, 5, 11)

    mid = Level(1, 12, 16, weights1, beside1)
    k1, f1, u1 = [(buf1.at[2 * a], buf1.at[2 * a + 1]) for a in range(3)]
    zeroed(u1[0])
    for slot, a in enumerate((0, 1, 2, 3, 5)):
        for place, part in enumerate((left, own, right)):
            for t in range(2):
                both = part[4 * slot + 2 * t : 4 * slot + 2 * t + 2].reshape(16, LANES)
                j = 4 * place + 2 * t
                buf1[a, j] = jnp.where(mid.y_odd_lane, pltpu.roll(both, 1, 1), both)
                buf1[a, j + 1] = jnp.where(mid.y_odd_lane, both, pltpu.roll(both, LANES - 1, 1))
    for j in range(12):
        i, side = 5 + j // 2, j % 2
        cell = jnp.where(level.odd, up2[1 - side][i], up2[side][i])
        grow1[j, pl.ds(0, 8, 2), :] = cell
        grow1[j, pl.ds(1, 8, 2), :] = cell
    for j in range(12):
        u1[1][j] = u1[1][j] + grow1[j]
    mid.setup(k1, 1, 11, 4 * wide - 4, 4 * size)
    mid.half(0, u1, f1, 1, 11)
    mid.half(1, u1, f1, 1, 11)
    mid.half(0, u1, f1, 2, 10)
    mid.half(1, u1, f1, 2, 10)

    fine = Level(0, 24, 32, weights0, beside0)
    k0, f0 = [(slab0.at[2 * a], slab0.at[2 * a + 1]) for a in range(2)]
    zeroed(u0.at[0])
    for i in range(5, 19):
        j, side = (i - 8 + 8) // 2, i % 2
        cell = jnp.where(mid.odd, u1[1 - side][j], u1[side][j])
        grow0[i, pl.ds(0, 16, 2), :] = cell
        grow0[i, pl.ds(1, 16, 2), :] = cell
    for i in range(5, 19):
        u0[1, i] = slab0[5, i] + grow0[i]
    up0 = (u0.at[0], u0.at[1])
    fine.setup(k0, 6, 18, 8 * wide - 8, 8 * size)
    fine.half(0, up0, f0, 6, 18)
    fine.half(1, up0, f0, 6, 18)
    fine.half(0, up0, f0, 7, 17)
    fine.half(1, up0, f0, 7, 17)
    odd8 = fine.odd[:8]

    def finish(i):
        grow0[0] = fine.defect(0, up0, f0, i)
        grow0[1] = fine.defect(1, up0, f0, i)
        rows = pl.ds(pl.multiple_of(8 * narrow, 8), 8)
        for out, first, second in (
            (pressure, u0[0, i, rows, :], u0[1, i, rows, :]),
            (residual, grow0[0, rows, :], grow0[1, rows, :]),
        ):
            out[2 * (i - 8)] = jnp.where(odd8, second, first)
            out[2 * (i - 8) + 1] = jnp.where(odd8, first, second)

    loop(8, 16, finish, group=1)


def f32(*shape):
    return jax.ShapeDtypeStruct(shape, jnp.float32)


def scratch(*shape):
    return pltpu.VMEM(shape, jnp.float32)


PARAMS = pltpu.CompilerParams(vmem_limit_bytes=48 * 1024 * 1024)


def shifted(block, distance):
    count = lax.axis_size("wide")
    if distance > 0:
        pairs = [(i, i + distance) for i in range(count - distance)]
    else:
        pairs = [(i, i + distance) for i in range(-distance, count)]
    return lax.ppermute(block, "wide", pairs)


def swapped(block, first):
    starts = range(first, lax.axis_size("wide") - 1, 2)
    return lax.ppermute(block, "wide", [pair for i in starts for pair in ((i, i + 1), (i + 1, i))])


def local(rhs, coefficient, guess):
    shape = (8, 8, LANES)
    odd = (lax.broadcasted_iota(jnp.int32, shape, 1) + lax.broadcasted_iota(jnp.int32, shape, 2)) % 2 == 1
    packed = jnp.where(odd, guess[0::2], guess[1::2])
    whole = lax.all_gather(jnp.concatenate([coefficient, rhs, packed], axis=0), "narrow")
    for_abroad, for_home = pl.pallas_call(
        spread_kernel,
        out_shape=(f32(4, 32, 8, LANES), f32(4, 32, 8, LANES)),
        compiler_params=PARAMS,
        name="spread",
    )(whole)
    abroad, home = swapped(for_abroad, 1), swapped(for_home, 0)
    slab0, send = pl.pallas_call(
        first_kernel,
        out_shape=(f32(6, 24, 32, LANES), f32(32, 8, LANES)),
        scratch_shapes=[
            scratch(2, 7, 24, 32, LANES),
            scratch(24, 32, LANES),
            scratch(2, 7, 12, 16, LANES),
            scratch(12, 16, LANES),
            scratch(6, 12, 16, LANES),
            scratch(24, 32, LANES),
            scratch(24, 32, LANES),
            scratch(12, 16, LANES),
        ],
        compiler_params=PARAMS,
        name="first",
    )(abroad, whole, home)
    near = (swapped(send, 0), send, swapped(send, 1))
    count = lax.axis_size("wide")
    out3, near_low, near_high = pl.pallas_call(
        second_kernel,
        out_shape=(f32(2 * count, LANES), f32(4, 4, 8, LANES), f32(4, 4, 8, LANES)),
        scratch_shapes=[scratch(6, 16, 8, LANES), scratch(2, 7, 16, 8, LANES), scratch(16, 8, LANES)],
        compiler_params=PARAMS,
        name="second",
    )(*near)
    far_left, far_right = shifted(near_high, 2), shifted(near_low, -2)
    data = lax.all_to_all(out3.reshape(count, 2, LANES), "wide", 0, 0).reshape(2 * count, LANES)
    return pl.pallas_call(
        third_kernel,
        out_shape=(f32(16, 8, LANES), f32(16, 8, LANES)),
        scratch_shapes=[
            scratch(count // 8, 8, LANES),
            scratch(3, count // 8, 8, LANES),
            scratch(7, count // 8, 8, LANES),
            scratch(2, 7, 16, 8, LANES),
            scratch(16, 8, LANES),
            scratch(6, 16, 8, LANES),
            scratch(2, 7, 12, 16, LANES),
            scratch(12, 16, LANES),
            scratch(6, 12, 16, LANES),
            scratch(12, 16, LANES),
            scratch(2, 7, 24, 32, LANES),
            scratch(24, 32, LANES),
            scratch(2, 24, 32, LANES),
            scratch(24, 32, LANES),
        ],
        compiler_params=PARAMS,
        name="third",
    )(data, far_left, *near, far_right, slab0)


def solution(mesh):
    spec = P("wide", "narrow", None)
    return jax.shard_map(
        local, mesh=mesh, in_specs=(spec, spec, spec), out_specs=(spec, spec), check_vma=False
    )
```

```python
import jax
import jax.numpy as jnp
from jax import lax
from jax.experimental import pallas as pl
from jax.experimental.pallas import tpu as pltpu
from jax.sharding import PartitionSpec as P

ITERS = 20
LANES = 128


class Level:
    def __init__(self, depth, pairs, rows, weights, beside):
        self.pairs, self.rows, self.step = pairs, rows, 1 << depth
        self.scale = 0.25**depth
        self.weights, self.beside = weights, beside
        z = lax.broadcasted_iota(jnp.int32, (rows, LANES), 0)
        lane = lax.broadcasted_iota(jnp.int32, (rows, LANES), 1)
        y = lane // self.step
        self.odd = (z + y) % 2 == 1
        self.y_odd = y % 2 == 1
        self.y_odd_lane = lane % 2 == 1
        self.z_last, self.z_first = z == rows - 1, z == 0
        self.y_last, self.y_first = lane >= LANES - self.step, lane < self.step

    def other(self, colour, ref, i):
        after, before = ref[i + 1], ref[i - 1]
        return jnp.where(self.odd, after, before) if colour == 0 else jnp.where(self.odd, before, after)

    def rolled(self, value):
        return (
            pltpu.roll(value, self.rows - 1, 0),
            pltpu.roll(value, 1, 0),
            pltpu.roll(value, LANES - self.step, 1),
            pltpu.roll(value, self.step, 1),
        )

    def setup(self, conduct, low, high, first, count):
        edges = (self.z_last, self.z_first, self.y_last, self.y_first)

        def body(i):
            inside = jnp.logical_and(first + i >= 0, first + i < count)
            for colour in (0, 1):
                own, near = conduct[colour][i], conduct[1 - colour][i]
                same = 0.5 * (own + near)
                across = 0.5 * (own + self.other(colour, conduct[1 - colour], i))
                total = same + across
                if colour == 0:
                    self.beside[i] = same
                self.weights[colour, 0, i] = across
                for slot, (edge, value) in enumerate(zip(edges, self.rolled(near))):
                    face = 0.5 * (own + jnp.where(edge, 0.0, value))
                    total = total + face
                    self.weights[colour, 1 + slot, i] = jnp.where(edge, 0.0, face)
                self.weights[colour, 5, i] = total
                total = jnp.where(total > 0.0, total, 1.0)
                self.weights[colour, 6, i] = jnp.where(inside, 1.0 / total, 0.0)

        loop(low, high, body)

    def around(self, colour, field, i):
        near = field[1 - colour][i]
        total = self.beside[i] * near + self.weights[colour, 0, i] * self.other(colour, field[1 - colour], i)
        for slot, value in enumerate(self.rolled(near)):
            total = total + self.weights[colour, 1 + slot, i] * value
        return total

    def half(self, colour, field, source, low, high):
        def body(i):
            fresh = source[colour][i] + self.around(colour, field, i)
            field[colour][i] = fresh * self.weights[colour, 6, i]

        loop(low, high, body)

    def start(self, field, source, low, high):
        def body(i):
            field[0][i] = source[0][i] * self.weights[0, 6, i]

        loop(low, high, body)

    def defect(self, colour, field, source, i):
        rest = source[colour][i] + self.around(colour, field, i) - self.weights[colour, 5, i] * field[colour][i]
        return rest if self.scale == 1.0 else self.scale * rest

    def pair_sum(self, value):
        return value + jnp.where(self.y_odd, pltpu.roll(value, self.step, 1), pltpu.roll(value, LANES - self.step, 1))


def loop(low, high, body, group=20):
    whole = (high - low) // group * group
    if whole:

        def several(step, carry):
            for k in range(group):
                body(low + step * group + k)
            return carry

        lax.fori_loop(0, whole // group, several, 0)
    for i in range(low + whole, high):
        body(i)


def halved(ref, i, rows):
    return ref[i, pl.ds(0, rows // 2, 2), :] + ref[i, pl.ds(1, rows // 2, 2), :]


def zeroed(*refs):
    for ref in refs:
        ref[...] = jnp.zeros(ref.shape, ref.dtype)


class Chosen:
    def __init__(self, which, yes, no):
        self.which, self.yes, self.no = which, yes, no

    def __getitem__(self, at):
        return jnp.where(self.which, self.yes[at], self.no[at])


def sides(abroad, home):
    even = lax.axis_index("wide") % 2 == 0
    return Chosen(even, abroad, home), Chosen(even, home, abroad)


def spread_kernel(whole, abroad, home):
    odd = lax.axis_index("wide") % 2
    for out, right in ((abroad, odd), (home, 1 - odd)):
        for n in range(4):
            out[n, 0:13] = whole[n, pl.ds(3 * right, 13)]
            out[n, 13:25] = whole[n, pl.ds(16 + 4 * right, 12)]
            out[n, 25:32] = whole[n, pl.ds(32 + right, 7)]


def first_kernel(abroad, own, home, slab, send, weights0, beside0, weights1, beside1, buf1, sums, sums1, tmp):
    wide = lax.axis_index("wide")
    left, right = sides(abroad, home)
    k0, f0, u0 = [(slab.at[2 * a], slab.at[2 * a + 1]) for a in range(3)]
    fine = Level(0, 24, 32, weights0, beside0)
    zeroed(u0[0])
    odd8 = fine.odd[:8]

    def row(base, n, kind, x):
        first, count = {"k": (0, 16), "f": (16, 16), "g": (32, 8)}[kind]
        start, kept = {"k": (0, 13), "f": (13, 12), "g": (25, 7)}[kind]
        if base == 8:
            return own[n, first + x]
        x = x - (count - kept) if base == 0 else x
        if x < 0 or x >= kept:
            return jnp.zeros((8, LANES), jnp.float32)
        return (left if base == 0 else right)[n, start + x]

    for n in range(4):
        z = slice(8 * n, 8 * n + 8)
        for i in range(1, 23):
            base, x = i // 8 * 8, 2 * (i % 8)
            for kind, target in (("k", k0), ("f", f0)):
                even, uneven = row(base, n, kind, x), row(base, n, kind, x + 1)
                target[0][i, z] = jnp.where(odd8, uneven, even)
                target[1][i, z] = jnp.where(odd8, even, uneven)
            u0[1][i, z] = row(base, n, "g", i % 8)
    fine.setup(k0, 2, 22, 8 * wide - 8, 8 * lax.axis_size("wide"))
    fine.half(0, u0, f0, 2, 22)
    fine.half(1, u0, f0, 2, 22)
    fine.half(0, u0, f0, 3, 21)
    fine.half(1, u0, f0, 3, 21)

    def down_k(i):
        sums[i] = fine.pair_sum(k0[0][i] + k0[1][i])

    loop(2, 22, down_k)

    def down_f(i):
        sums1[i] = fine.pair_sum(fine.defect(0, u0, f0, i) + fine.defect(1, u0, f0, i))

    loop(4, 20, down_f)

    mid = Level(1, 12, 16, weights1, beside1)
    k1, f1, u1 = [(buf1.at[2 * a], buf1.at[2 * a + 1]) for a in range(3)]
    zeroed(u1[0], u1[1])

    def pack(target, source, factor, j):
        even, uneven = factor * halved(source, 2 * j, 32), factor * halved(source, 2 * j + 1, 32)
        target[0][j] = jnp.where(mid.odd, uneven, even)
        target[1][j] = jnp.where(mid.odd, even, uneven)

    loop(1, 11, lambda j: pack(k1, sums, 0.125, j))
    loop(2, 10, lambda j: pack(f1, sums1, 0.125 / 0.25, j))
    mid.setup(k1, 2, 10, 4 * wide - 4, 4 * lax.axis_size("wide"))
    mid.start(u1, f1, 2, 10)
    mid.half(1, u1, f1, 2, 10)
    mid.half(0, u1, f1, 3, 9)
    mid.half(1, u1, f1, 3, 9)
    for slot, a in enumerate((0, 1, 2, 3, 5)):
        for t in range(2):
            both = jnp.where(mid.y_odd_lane, buf1[a, 5 + 2 * t], buf1[a, 4 + 2 * t])
            send[4 * slot + 2 * t : 4 * slot + 2 * t + 2] = both.reshape(2, 8, LANES)

    z8 = lax.broadcasted_iota(jnp.int32, (8, LANES), 0)
    lane8 = lax.broadcasted_iota(jnp.int32, (8, LANES), 1)
    odd2 = (z8 + lane8 // 4) % 2 == 1

    def write(base, cells):
        for t in range(len(cells) // 2):
            even, uneven = cells[2 * t], cells[2 * t + 1]
            send[base + t] = jnp.where(odd2, uneven, even)
            send[base + len(cells) // 2 + t] = jnp.where(odd2, even, uneven)

    for x in range(8):
        tmp[x] = mid.pair_sum(k1[0][2 + x] + k1[1][2 + x])
    for x in range(4):
        j = 4 + x
        tmp[8 + x] = mid.pair_sum(mid.defect(0, u1, f1, j) + mid.defect(1, u1, f1, j))
    write(20, [0.125 * halved(tmp, x, 16) for x in range(8)])
    write(28, [0.125 / 0.0625 * halved(tmp, 8 + x, 16) for x in range(4)])


def place_two(slab, part, base):
    for c in range(2):
        for t in range(4):
            slab[c, base - 1 + t] = part[20 + 4 * c + t]
        for t in range(2):
            slab[2 + c, base + t] = part[28 + 2 * c + t]


def second_kernel(home, own, abroad, out, near_low, near_high, slab, weights, beside):
    wide = lax.axis_index("wide")
    left, right = sides(abroad, home)
    level = Level(2, 16, 8, weights, beside)
    k, f, u = [(slab.at[2 * a], slab.at[2 * a + 1]) for a in range(3)]
    zeroed(slab)
    place_two(slab, left, 5)
    place_two(slab, right, 9)
    place_two(slab, own, 7)
    for a in range(4):
        near_high[a] = slab[a, 5:9]
        near_low[a] = slab[a, 7:11]
    level.setup(k, 5, 11, 2 * wide - 7, 2 * lax.axis_size("wide"))
    level.start(u, f, 5, 11)
    level.half(1, u, f, 5, 11)
    level.half(0, u, f, 6, 10)
    level.half(1, u, f, 6, 10)
    lane = lax.broadcasted_iota(jnp.int32, (8, LANES), 1)
    row = lax.broadcasted_iota(jnp.int32, (8, LANES), 0)
    pick = 8 * (lane % 16)
    keep = row == 2 * ((lane // 16) % 4)

    def compact(values):
        outs = []
        for value in values:
            value = level.pair_sum(value)
            value = 0.125 * (value + pltpu.roll(value, 7, 0))
            value = jnp.take_along_axis(value, pick, axis=1)
            outs.append(jnp.sum(jnp.where(keep, value, 0.0), axis=0, keepdims=True))
        return jnp.where(lane[:1] < 64, outs[0], outs[1])

    source = compact([level.defect(0, u, f, i) + level.defect(1, u, f, i) for i in (7, 8)])
    conduct = compact([k[0][i] + k[1][i] for i in (7, 8)])
    both = jnp.where(row % 2 == 0, source, conduct)
    for w in range(out.shape[0] // 8):
        out[8 * w : 8 * w + 8] = both


def coarsest(data, answer, vectors, faces, iters):
    remain, search, image = (vectors.at[a] for a in range(3))
    parts = data.shape[0] // 16
    scale = 0.25**3
    row = lax.broadcasted_iota(jnp.int32, (8, LANES), 0)
    lane = lax.broadcasted_iota(jnp.int32, (8, LANES), 1)
    y, z, x = lane % 16, (lane // 16) % 4, lane // 64

    def around(values):
        swapped = [pltpu.roll(value, 64, 1) for value in values]
        before = [pltpu.roll(swapped[-1], 1, 0)] + swapped[:-1]
        after = swapped[1:] + [pltpu.roll(swapped[0], 7, 0)]
        return [
            (
                swapped[v],
                jnp.where(x == 0, before[v], after[v]),
                pltpu.roll(value, LANES - 16, 1),
                pltpu.roll(value, 16, 1),
                pltpu.roll(value, LANES - 1, 1),
                pltpu.roll(value, 1, 1),
            )
            for v, value in enumerate(values)
        ]

    def total(values):
        while len(values) > 1:
            values = [a + b for a, b in zip(values[::2], values[1::2])]
        value = values[0]
        for shift in (4, 2, 1):
            value = value + pltpu.roll(value, shift, 0)
        return jnp.sum(value, axis=1, keepdims=True)

    source = [data[pl.ds(2 * v, 8, 2 * parts), :] for v in range(parts)]
    conduct = [data[pl.ds(2 * v + 1, 8, 2 * parts), :] for v in range(parts)]
    for v, near in enumerate(around(conduct)):
        end = None
        if v == 0:
            end = jnp.logical_and(x == 0, row == 0)
        if v == parts - 1:
            end = jnp.logical_and(x == 1, row == 7)
        diagonal = None
        for slot, (edge, value) in enumerate(zip((None, end, z == 3, z == 0, y == 15, y == 0), near)):
            if edge is not None:
                value = jnp.where(edge, 0.0, value)
            face = (0.5 * scale) * (conduct[v] + value)
            diagonal = face if diagonal is None else diagonal + face
            faces[slot, v] = face if edge is None else jnp.where(edge, 0.0, face)
        faces[6, v] = diagonal

    def operate(values):
        return [
            faces[6, v] * values[v] - sum(faces[slot, v] * value for slot, value in enumerate(near))
            for v, near in enumerate(around(values))
        ]

    def products(values, images):
        return total([a * a for a in values]), total([a * b for a, b in zip(values, images)])

    def advance(step, carry):
        rest = [remain[v] for v in range(parts)]
        images = operate(rest)
        norm = total([a * a for a in rest])
        power = total([a * b for a, b in zip(rest, images)])
        if carry is None:
            for v in range(parts):
                answer[v] = jnp.zeros_like(rest[v])
        else:
            beta = norm * carry[0]
            power = power - beta * beta * carry[1]
        alpha = norm / power
        for v in range(parts):
            now, one = rest[v], images[v]
            if carry is not None:
                now, one = now + beta * search[v], one + beta * image[v]
            search[v], image[v] = now, one
            answer[v] = answer[v] + alpha * now
            remain[v] = rest[v] - alpha * one
        return 1.0 / norm, power

    for v, value in enumerate(source):
        remain[v] = value
    carry = None
    for step in range(iters):
        carry = advance(step, carry)


def third_kernel(data, far_left, home, own, abroad, far_right, slab0, pressure, residual, answer, vectors, faces,
                 weights2, beside2, slab2, weights1, beside1, buf1, grow1, weights0, beside0, u0, grow0):
    wide, narrow = lax.axis_index("wide"), lax.axis_index("narrow")
    left, right = sides(abroad, home)
    size = lax.axis_size("wide")
    level = Level(2, 16, 8, weights2, beside2)
    k, f, up2 = [(slab2.at[2 * a], slab2.at[2 * a + 1]) for a in range(3)]
    zeroed(slab2)
    for a in range(4):
        slab2[a, 1:5] = far_left[a]
        slab2[a, 11:15] = far_right[a]
    place_two(slab2, left, 5)
    place_two(slab2, right, 9)
    place_two(slab2, own, 7)
    level.setup(k, 1, 15, 2 * wide - 7, 2 * size)
    level.start(up2, f, 1, 15)
    level.half(1, up2, f, 2, 14)
    level.half(0, up2, f, 2, 14)
    level.half(1, up2, f, 3, 13)

    coarsest(data, answer, vectors, faces, ITERS)
    lane = lax.broadcasted_iota(jnp.int32, (8, LANES), 1)
    row = lax.broadcasted_iota(jnp.int32, (8, LANES), 0)
    where_from = (row // 2) * 16 + lane // 8
    parts = answer.shape[0]
    for t in range(5):
        at = wide - 2 + t
        inside = jnp.logical_and(at >= 0, at < size)
        at = jnp.clip(at, 0, size - 1)
        line = jnp.where(row == at // parts, answer[at % parts], 0.0)
        line = jnp.where(inside, jnp.sum(line, axis=0, keepdims=True), 0.0)
        line = jnp.broadcast_to(line, (8, LANES))
        for half in range(2):
            i = 3 + 2 * t + half
            slab2[5, i] = slab2[5, i] + jnp.take_along_axis(line, where_from + 64 * half, axis=1)
    level.half(0, up2, f, 3, 13)
    level.half(1, up2, f, 4, 12)
    level.half(0, up2, f, 4, 12)
    level.half(1, up2, f, 5, 11)

    mid = Level(1, 12, 16, weights1, beside1)
    k1, f1, u1 = [(buf1.at[2 * a], buf1.at[2 * a + 1]) for a in range(3)]
    zeroed(u1[0])
    for slot, a in enumerate((0, 1, 2, 3, 5)):
        for place, part in enumerate((left, own, right)):
            for t in range(2):
                both = part[4 * slot + 2 * t : 4 * slot + 2 * t + 2].reshape(16, LANES)
                j = 4 * place + 2 * t
                buf1[a, j] = jnp.where(mid.y_odd_lane, pltpu.roll(both, 1, 1), both)
                buf1[a, j + 1] = jnp.where(mid.y_odd_lane, both, pltpu.roll(both, LANES - 1, 1))
    for j in range(12):
        i, side = 5 + j // 2, j % 2
        cell = jnp.where(level.odd, up2[1 - side][i], up2[side][i])
        grow1[j, pl.ds(0, 8, 2), :] = cell
        grow1[j, pl.ds(1, 8, 2), :] = cell
    for j in range(12):
        u1[1][j] = u1[1][j] + grow1[j]
    mid.setup(k1, 1, 11, 4 * wide - 4, 4 * size)
    mid.half(0, u1, f1, 1, 11)
    mid.half(1, u1, f1, 1, 11)
    mid.half(0, u1, f1, 2, 10)
    mid.half(1, u1, f1, 2, 10)

    fine = Level(0, 24, 32, weights0, beside0)
    k0, f0 = [(slab0.at[2 * a], slab0.at[2 * a + 1]) for a in range(2)]
    zeroed(u0.at[0])
    for i in range(5, 19):
        j, side = (i - 8 + 8) // 2, i % 2
        cell = jnp.where(mid.odd, u1[1 - side][j], u1[side][j])
        grow0[i, pl.ds(0, 16, 2), :] = cell
        grow0[i, pl.ds(1, 16, 2), :] = cell
    for i in range(5, 19):
        u0[1, i] = slab0[5, i] + grow0[i]
    up0 = (u0.at[0], u0.at[1])
    fine.setup(k0, 6, 18, 8 * wide - 8, 8 * size)
    fine.half(0, up0, f0, 6, 18)
    fine.half(1, up0, f0, 6, 18)
    fine.half(0, up0, f0, 7, 17)
    fine.half(1, up0, f0, 7, 17)
    odd8 = fine.odd[:8]

    def finish(i):
        grow0[0] = fine.defect(0, up0, f0, i)
        grow0[1] = fine.defect(1, up0, f0, i)
        rows = pl.ds(pl.multiple_of(8 * narrow, 8), 8)
        for out, first, second in (
            (pressure, u0[0, i, rows, :], u0[1, i, rows, :]),
            (residual, grow0[0, rows, :], grow0[1, rows, :]),
        ):
            out[2 * (i - 8)] = jnp.where(odd8, second, first)
            out[2 * (i - 8) + 1] = jnp.where(odd8, first, second)

    loop(8, 16, finish, group=1)


def f32(*shape):
    return jax.ShapeDtypeStruct(shape, jnp.float32)


def scratch(*shape):
    return pltpu.VMEM(shape, jnp.float32)


PARAMS = pltpu.CompilerParams(vmem_limit_bytes=48 * 1024 * 1024)


def shifted(block, distance):
    count = lax.axis_size("wide")
    if distance > 0:
        pairs = [(i, i + distance) for i in range(count - distance)]
    else:
        pairs = [(i, i + distance) for i in range(-distance, count)]
    return lax.ppermute(block, "wide", pairs)


def swapped(block, first):
    starts = range(first, lax.axis_size("wide") - 1, 2)
    return lax.ppermute(block, "wide", [pair for i in starts for pair in ((i, i + 1), (i + 1, i))])


def local(rhs, coefficient, guess):
    shape = (8, 8, LANES)
    odd = (lax.broadcasted_iota(jnp.int32, shape, 1) + lax.broadcasted_iota(jnp.int32, shape, 2)) % 2 == 1
    packed = jnp.where(odd, guess[0::2], guess[1::2])
    whole = lax.all_gather(jnp.concatenate([coefficient, rhs, packed], axis=0), "narrow")
    for_abroad, for_home = pl.pallas_call(
        spread_kernel,
        out_shape=(f32(4, 32, 8, LANES), f32(4, 32, 8, LANES)),
        compiler_params=PARAMS,
        name="spread",
    )(whole)
    abroad, home = swapped(for_abroad, 1), swapped(for_home, 0)
    slab0, send = pl.pallas_call(
        first_kernel,
        out_shape=(f32(6, 24, 32, LANES), f32(32, 8, LANES)),
        scratch_shapes=[
            scratch(2, 7, 24, 32, LANES),
            scratch(24, 32, LANES),
            scratch(2, 7, 12, 16, LANES),
            scratch(12, 16, LANES),
            scratch(6, 12, 16, LANES),
            scratch(24, 32, LANES),
            scratch(24, 32, LANES),
            scratch(12, 16, LANES),
        ],
        compiler_params=PARAMS,
        name="first",
    )(abroad, whole, home)
    near = (swapped(send, 0), send, swapped(send, 1))
    count = lax.axis_size("wide")
    out3, near_low, near_high = pl.pallas_call(
        second_kernel,
        out_shape=(f32(2 * count, LANES), f32(4, 4, 8, LANES), f32(4, 4, 8, LANES)),
        scratch_shapes=[scratch(6, 16, 8, LANES), scratch(2, 7, 16, 8, LANES), scratch(16, 8, LANES)],
        compiler_params=PARAMS,
        name="second",
    )(*near)
    far_left, far_right = shifted(near_high, 2), shifted(near_low, -2)
    data = lax.all_to_all(out3.reshape(count, 2, LANES), "wide", 0, 0).reshape(2 * count, LANES)
    return pl.pallas_call(
        third_kernel,
        out_shape=(f32(16, 8, LANES), f32(16, 8, LANES)),
        scratch_shapes=[
            scratch(count // 8, 8, LANES),
            scratch(3, count // 8, 8, LANES),
            scratch(7, count // 8, 8, LANES),
            scratch(2, 7, 16, 8, LANES),
            scratch(16, 8, LANES),
            scratch(6, 16, 8, LANES),
            scratch(2, 7, 12, 16, LANES),
            scratch(12, 16, LANES),
            scratch(6, 12, 16, LANES),
            scratch(12, 16, LANES),
            scratch(2, 7, 24, 32, LANES),
            scratch(24, 32, LANES),
            scratch(2, 24, 32, LANES),
            scratch(24, 32, LANES),
        ],
        compiler_params=PARAMS,
        name="third",
    )(data, far_left, *near, far_right, slab0)


def solution(mesh):
    spec = P("wide", "narrow", None)
    return jax.shard_map(
        local, mesh=mesh, in_specs=(spec, spec, spec), out_specs=(spec, spec), check_vma=False
    )
```
